512 devices in a mesh: rep: 8 (over x_lo, y), fsdp: 64 (over x_hi, z, core).
Axes of the slice: x: 4 (x_hi: 2, x_lo: 2; x = x_hi * 2 + x_lo), y: 4, z: 16, core: 2. Of those that a mesh axis runs over, the one named last changes fastest.
Arguments:
- hidden: bfloat16 [131072, 5120], P(('rep', 'fsdp')), may hold values from -6 to 6
- weight: bfloat16 [640, 64, 128], P('fsdp'), may hold values from -0.078125 to 0.078125
- momentum: float32 [8, 640, 64, 128], P('rep', 'fsdp'), may hold values from -6 to 6
- gradient: bfloat16 [8, 640, 64, 128], P('rep', 'fsdp'), may hold values from -6 to 6
- indices: int32 [8, 1280, 32], P('rep', 'fsdp'), may hold values from 0 to 4095, as said below
- counts: int32 [8, 1280], P('rep', 'fsdp'), may hold values from 1 to 32, as said below
Outputs:
- key_states: bfloat16 [131072, 1024], P(('rep', 'fsdp'))
- update: bfloat16 [640, 64, 128], P('fsdp', 'rep')
- new_momentum: float32 [8, 640, 64, 128], P('rep', 'fsdp')
The draws below stay inside these ranges and needn't reach their ends.
Inputs may be any that keep to these rules, and one draw needn't show every extreme that they name: `indices`: the 32 numbers of one replica's block differ from one another. `counts`: some block of every replica keeps all 32.
All inputs are finite; a program needn't handle non-finite values.
Results may differ from the reference program's by a relative error of at most 0.0095.
Values may be sent and summed in bfloat16 or wider, within the bound.
No kernel may reach another device: no remote copies, remote signals or barrier semaphores. Data moves between devices by JAX's collectives and lax.ppermute only.
A program may use at most 128 MiB of HBM per device.

```python
import jax
import jax.numpy as jnp
from jax import lax

D = 5120
KV = 1024
CH = 64
TOPK = 32
TOK_DEV = 256
TILES = 640
SPANS = 1280
TOKEN_TOTAL = 131072
N_REP = 8


def draw_indices(key, part):
    key = jax.random.fold_in(key, 11)
    replica_keys = jax.random.split(key, N_REP)

    def one_replica(sub_key):
        scores = jax.random.randint(sub_key, (SPANS, CH * CH), 0, 2 ** 18)
        scores = scores * (CH * CH) + jnp.arange(CH * CH, dtype=jnp.int32)[None, :]
        return lax.top_k(scores, TOPK)[1].astype(jnp.int32)
    return lax.map(one_replica, replica_keys)


def draw_counts(key, part):
    key = jax.random.fold_in(key, 23)
    first_key, second_key = jax.random.split(key)
    drawn = jax.random.randint(first_key, (N_REP, SPANS), 1, TOPK + 1)
    complete_block = jax.random.randint(second_key, (N_REP, 1), 0, SPANS)
    position = jnp.arange(SPANS, dtype=jnp.int32)[None, :]
    return jnp.where(position == complete_block, TOPK, drawn).astype(jnp.int32)


def levels(rng, dims, cuts, least, largest):
    factor_of = 1.0
    for dim, blocks in cuts:
        steps = jax.random.uniform(jax.random.fold_in(jax.random.fold_in(rng, 6), dim), (blocks,), jnp.float32, least / len(cuts), largest / len(cuts))
        factor_of = factor_of * jnp.repeat(jnp.exp(steps), dims[dim] // blocks).reshape((-1,) + (1,) * (len(dims) - 1 - dim))
    return factor_of


def gaussian(own_key, shape, scale, most, cuts=(), kind=jnp.bfloat16):
    loudness = levels(own_key, shape, cuts, -0.22, 0.18) if cuts else 1.0
    values = jax.random.normal(own_key, shape, jnp.float32) * scale * loudness
    return jnp.minimum(jnp.maximum(values, -most), most).astype(kind)


def setup_inputs(seed: int = 0) -> dict:
    arg_keys = jax.random.split(jax.random.key(seed), 7)
    hidden = gaussian(arg_keys[0], (TOKEN_TOTAL, D), 1.0, 6.0, ((0, 512),))
    weight = gaussian(arg_keys[1], (TILES, CH, 2 * CH), D ** -0.5, 0.078125, ((0, 64),))
    momentum = gaussian(arg_keys[2], (N_REP, TILES, CH, 2 * CH), 1.0, 6.0, ((0, 8), (1, 64)), jnp.float32)
    gradient = gaussian(arg_keys[3], (N_REP, TILES, CH, 2 * CH), 1.0, 6.0, ((0, 8), (1, 64)))
    indices = draw_indices(jax.random.fold_in(arg_keys[6], 71), 0)
    counts = draw_counts(jax.random.fold_in(arg_keys[6], 71), 0)
    return dict(hidden=hidden, weight=weight, momentum=momentum, gradient=gradient, indices=indices, counts=counts)


decay_rate = 0.999
step_size = 0.01
tiny_eps = 1e-06

def dct_table(length):
    wave_number = jnp.arange(length, dtype=jnp.float32)[:, None]
    position = jnp.arange(length, dtype=jnp.float32)[None, :]
    dct_rows = jnp.cos(jnp.pi * (2.0 * position + 1.0) * wave_number / (2.0 * length)) * jnp.sqrt(2.0 / length)
    return jnp.where(wave_number == 0.0, dct_rows * jnp.sqrt(0.5), dct_rows)

def to_spectrum(blocks, dct_rows):
    return jnp.einsum('ka,...ab,lb->...kl', dct_rows, blocks, dct_rows, precision=lax.Precision.HIGHEST)

def from_spectrum(tile_frequency_coefficients, dct_rows):
    return jnp.einsum('ka,...kl,lb->...ab', dct_rows, tile_frequency_coefficients, dct_rows, precision=lax.Precision.HIGHEST)

def reference(hidden, weight, momentum, gradient, indices, counts):
    dct_rows = dct_table(CH)
    moment = decay_rate * momentum + gradient.astype(jnp.float32)
    blocks = moment.reshape(N_REP, TILES, CH, 2, CH).transpose(0, 1, 3, 2, 4).reshape(N_REP, SPANS, CH, CH)
    tile_frequency_coefficients = to_spectrum(blocks, dct_rows).reshape(N_REP, SPANS, CH * CH)
    picked = jnp.take_along_axis(tile_frequency_coefficients, indices, axis=2)
    is_live = jnp.arange(TOPK, dtype=jnp.int32)[None, None, :] < counts[:, :, None]
    kept_values = jnp.where(is_live, picked, jnp.zeros_like(picked))
    replica_rows = jnp.arange(N_REP, dtype=jnp.int32)[:, None, None]
    span_rows = jnp.arange(SPANS, dtype=jnp.int32)[None, :, None]
    own_spectra = jnp.zeros((N_REP, SPANS, CH * CH), jnp.float32).at[replica_rows, span_rows, indices].add(kept_values)
    own_spectra = own_spectra.reshape(N_REP, SPANS, CH, CH)
    estimate = from_spectrum(own_spectra, dct_rows)
    new_blocks = blocks - estimate
    new_momentum = new_blocks.reshape(N_REP, TILES, 2, CH, CH).transpose(0, 1, 3, 2, 4).reshape(N_REP, TILES, CH, 2 * CH)
    shared = lax.optimization_barrier(jnp.sum(own_spectra, axis=0)) / N_REP
    raw_descent_direction = from_spectrum(shared, dct_rows)
    span_scale = jnp.sqrt(lax.optimization_barrier(jnp.mean(raw_descent_direction * raw_descent_direction, axis=(1, 2), keepdims=True)) + tiny_eps)
    update = jnp.tanh(raw_descent_direction / span_scale).astype(jnp.bfloat16)
    update = update.reshape(TILES, 2, CH, CH).transpose(0, 2, 1, 3).reshape(TILES, CH, 2 * CH)
    revised_parameters = (weight.astype(jnp.float32) - step_size * update.astype(jnp.float32)).astype(jnp.bfloat16)
    matrix = revised_parameters.reshape(KV // (2 * CH), D // CH, CH, 2 * CH).transpose(1, 2, 0, 3).reshape(D, KV)

    def project(row_block):
        return jnp.dot(row_block, matrix, preferred_element_type=jnp.float32).astype(jnp.bfloat16)
    key_states = lax.map(project, hidden.reshape(TOKEN_TOTAL // TOK_DEV, TOK_DEV, D)).reshape(TOKEN_TOTAL, KV)
    return (key_states, update, new_momentum)
```

```python
import functools

import jax
import jax.numpy as jnp
import numpy as np
from jax import lax
from jax.experimental import pallas as pl
from jax.experimental.pallas import tpu as pltpu
from jax.sharding import Mesh, PartitionSpec as P

decay_rate = 0.999
step_size = 0.01
tiny_eps = 1e-06
SIDE = 64
exact = lax.Precision.HIGHEST
f32 = jnp.float32
bf16 = jnp.bfloat16
axes = ("xl", "y", "xh", "z", "c")
VMEM_LIMIT = 48 * 1024 * 1024


def tables():
    k = np.arange(SIDE)[:, None]
    n = np.arange(SIDE)[None, :]
    rows = np.cos(np.pi * (2 * n + 1) * k / (2 * SIDE)) * np.sqrt(2.0 / SIDE)
    rows[0] *= np.sqrt(0.5)
    pair = np.zeros((2 * SIDE, 2 * SIDE))
    pair[:SIDE, :SIDE] = rows
    pair[SIDE:, SIDE:] = rows
    ones = np.kron(np.eye(2), np.ones((SIDE, SIDE)))
    return rows.astype(np.float32), pair.astype(np.float32), ones.astype(np.float32)


def dot(a, b, dims=((1,), (0,)), precision=exact):
    return lax.dot_general(a, b, (dims, ((), ())), precision=precision, preferred_element_type=f32)


def one_hots(index_row):
    n = index_row.shape[1]
    lane = lax.broadcasted_iota(jnp.int32, (1, n), 1)
    row = index_row >> 6
    column = (index_row & 63) + jnp.where((lane & 63) >= 32, SIDE, 0)
    row_hot = jnp.where(lax.broadcasted_iota(jnp.int32, (SIDE, n), 0) == row, 1.0, 0.0).astype(f32)
    column_hot = jnp.where(
        lax.broadcasted_iota(jnp.int32, (2 * SIDE, n), 0) == column, 1.0, 0.0
    ).astype(f32)
    return row_hot, column_hot


def split_hidden_kernel(hidden, parts):
    for j in range(8):
        for half in range(2):
            piece = hidden[:, j * 640 + half * 320 : j * 640 + half * 320 + 320]
            for twin in range(2):
                parts[half, twin, :, j * 320 : j * 320 + 320] = piece


def values_kernel(momentum, gradient, indices, live, rows, pair, values):
    tiles = momentum.shape[1]
    table, wide = rows[...], pair[...]
    for t in range(tiles):
        moment = decay_rate * momentum[0, t] + gradient[0, t].astype(f32)
        spectrum = dot(dot(table, moment), wide, ((1,), (1,)))
        row_hot, column_hot = one_hots(indices[t : t + 1, :])
        picked = dot(spectrum, row_hot, ((0,), (0,)))
        value = jnp.sum(picked * column_hot, axis=0, keepdims=True)
        values[t : t + 1, :] = jnp.where(live[t : t + 1, :] > 0, value, 0.0)


def momentum_kernel(momentum, gradient, indices, values, rows, pair, out):
    tiles = momentum.shape[1]
    table, wide = rows[...], pair[...]
    for t in range(tiles):
        moment = decay_rate * momentum[0, t] + gradient[0, t].astype(f32)
        row_hot, column_hot = one_hots(indices[t : t + 1, :])
        spectrum = dot(row_hot * values[t : t + 1, :], column_hot, ((1,), (1,)))
        out[0, t] = moment - dot(dot(table, spectrum, ((0,), (0,))), wide)


def update_kernel(place, got_values, got_indices, weight, rows, pair, ones, update, pieces, raw, tanhs):
    replicas, tiles = got_values.shape[0], got_values.shape[1]
    table, wide = rows[...], pair[...]
    sums = []
    for t in range(tiles):
        index_row = jnp.concatenate([got_indices[r, t : t + 1, :] for r in range(replicas)], axis=1)
        value_row = jnp.concatenate([got_values[r, t : t + 1, :] for r in range(replicas)], axis=1)
        row_hot, column_hot = one_hots(index_row)
        shared = dot(row_hot * value_row, column_hot, ((1,), (1,))) / replicas
        flat = dot(dot(table, shared, ((0,), (0,))), wide)
        raw[t] = flat
        sums.append(jnp.sum(flat * flat, axis=0, keepdims=True))
    energy = dot(jnp.concatenate(sums, axis=0), ones[...])
    scale = jnp.sqrt(energy / (SIDE * SIDE) + tiny_eps)
    for t in range(tiles):
        tanhs[t] = jnp.tanh(raw[t] / scale[t : t + 1, :])
    own_rows = pl.multiple_of(place[0] * 8, 8)
    for t in range(tiles):
        update[t] = tanhs[t, pl.ds(own_rows, 8), :].astype(bf16)
    first_tile = place[1] * (tiles // 2)
    first_row = pl.multiple_of(place[2] * 16, 16)
    for t in range(tiles // 2):
        moved = tanhs[first_tile + t, pl.ds(first_row, 16), :].astype(bf16).astype(f32)
        old = weight[first_tile + t, pl.ds(first_row, 16), :].astype(f32)
        new = (old - step_size * moved).astype(bf16)
        for z in range(pieces.shape[0]):
            pieces[z, t] = new


def project_kernel(place, hidden, own, other, out, matrix):
    @pl.when(pl.program_id(0) == 0)
    def _():
        for source, core in ((own, place[0]), (other, 1 - place[0])):
            for z in range(16):
                start = pl.multiple_of((z % 4 * 2 + core) * 320, 64)
                for t in range(5):
                    for y in range(4):
                        matrix[pl.ds(start + t * 64 + y * 16, 16), z // 4 * 128 : z // 4 * 128 + 128] = source[y, z, t]

    out[0] = jnp.dot(hidden[0], matrix[...], preferred_element_type=f32).astype(bf16)


def call(kernel, out_shape, *args, scratch=(), flops=0, moved=0, **more):
    return pl.pallas_call(
        kernel,
        out_shape=out_shape,
        scratch_shapes=list(scratch),
        compiler_params=pltpu.CompilerParams(vmem_limit_bytes=VMEM_LIMIT),
        cost_estimate=pl.CostEstimate(flops=flops, bytes_accessed=moved, transcendentals=0),
        **more,
    )(*args)


def shards(hidden, weight, momentum, gradient, indices, counts):
    tiles = weight.shape[0]
    kept = indices.shape[2]
    rows, pair, ones = (jnp.asarray(a) for a in tables())
    xl, y, c = lax.axis_index("xl"), lax.axis_index("y"), lax.axis_index("c")
    vm, sm = pl.BlockSpec(memory_space=pltpu.VMEM), pl.BlockSpec(memory_space=pltpu.SMEM)

    with jax.named_scope("hidden_exchange"):
        parts = call(
            split_hidden_kernel,
            jax.ShapeDtypeStruct((2, 2, 256, 2560), bf16),
            hidden,
            moved=8 * 2**20,
            in_specs=[vm],
            out_specs=vm,
        )
        tokens = lax.all_to_all(parts.reshape(4, 256, 2560), ("xl", "xh"), 0, 0)

    with jax.named_scope("own_values"):
        live = (jnp.arange(kept, dtype=jnp.int32)[None, :] < counts[0][:, None]).astype(jnp.int32)
        live = live.reshape(tiles, 2 * kept)
        places = indices[0].reshape(tiles, 2 * kept)
        values = call(
            values_kernel,
            jax.ShapeDtypeStruct((tiles, 2 * kept), f32),
            momentum, gradient, places, live, rows, pair,
            flops=2**28, moved=2**19,
            in_specs=[vm] * 6,
            out_specs=vm,
        )

    with jax.named_scope("replica_exchange"):
        sent = jnp.stack([values, places.astype(f32)])
        got = lax.all_to_all(jnp.broadcast_to(sent, (8,) + sent.shape), ("xl", "y"), 0, 0)

    with jax.named_scope("new_weight"):
        update, pieces = call(
            update_kernel,
            (jax.ShapeDtypeStruct((tiles, 8, 128), bf16), jax.ShapeDtypeStruct((16, tiles // 2, 16, 128), bf16)),
            jnp.stack([xl * 4 + y, xl, y]).astype(jnp.int32),
            got[:, 0], got[:, 1].astype(jnp.int32), weight, rows, pair, ones,
            scratch=[pltpu.VMEM((tiles, SIDE, 128), f32)] * 2,
            flops=2**28, moved=2**19,
            in_specs=[sm] + [vm] * 6,
            out_specs=(vm, vm),
        )

    with jax.named_scope("weight_exchange"):
        along_z = lax.all_to_all(pieces, "z", 0, 0)
        along_y = lax.all_to_all(jnp.broadcast_to(along_z, (4,) + along_z.shape), "y", 0, 0)
        other = lax.ppermute(along_y, "c", [(0, 1), (1, 0)])

    with jax.named_scope("projection"):
        whole = pl.BlockSpec((4, 16, 5, 16, 128), lambda i: (0, 0, 0, 0, 0))
        partial = call(
            project_kernel,
            jax.ShapeDtypeStruct((4, 256, 512), bf16),
            c.reshape(1).astype(jnp.int32), tokens, along_y, other,
            scratch=[pltpu.VMEM((2560, 512), bf16)],
            flops=2 * 1024 * 2560 * 512, moved=10 * 2**20,
            grid=(4,),
            in_specs=[sm, pl.BlockSpec((1, 256, 2560), lambda i: (i, 0, 0)), whole, whole],
            out_specs=pl.BlockSpec((1, 256, 512), lambda i: (i, 0, 0)),
        )

    with jax.named_scope("output_exchange"):
        back = lax.all_to_all(partial, ("xl", "xh"), 0, 0).astype(f32)
        back = back.reshape(2, 2, 256, 512).sum(0).astype(bf16)
        keys = jnp.concatenate([back[0], back[1]], axis=1)

    with jax.named_scope("momentum"):
        new_momentum = call(
            momentum_kernel,
            jax.ShapeDtypeStruct(momentum.shape, f32),
            momentum, gradient, places, values, rows, pair,
            flops=2**28, moved=2**20,
            in_specs=[vm] * 6,
            out_specs=vm,
        )
    return (keys, update, new_momentum)


def solution(mesh):
    fine = Mesh(mesh.devices.reshape(2, 4, 2, 16, 2), axes)
    rep, group = ("xl", "y"), ("xh", "z", "c")
    in_specs = (
        P(axes[:2] + axes[2:], None),
        P(group, None, None),
        P(rep, group, None, None),
        P(rep, group, None, None),
        P(rep, group, None),
        P(rep, group),
    )
    out_specs = (P(axes, None), P(group, rep, None), P(rep, group, None, None))
    return jax.shard_map(shards, mesh=fine, in_specs=in_specs, out_specs=out_specs, check_vma=False)
```

```python
import jax
import jax.numpy as jnp
import numpy as np
from jax import lax
from jax.experimental import pallas as pl
from jax.experimental.pallas import tpu as pltpu
from jax.sharding import Mesh, PartitionSpec as P

decay_rate = 0.999
step_size = 0.01
tiny_eps = 1e-06
SIDE = 64
PAIR = 128
f32 = jnp.float32
bf16 = jnp.bfloat16
axes = ("xl", "y", "xh", "z", "c")
VMEM_LIMIT = 40 * 1024 * 1024
WIDE_T, WIDE, BLOCK_ONES = 0, 2, 4
HALF = 1280


def split(a):
    high = a.astype(bf16)
    return high, (a - high.astype(f32)).astype(bf16)


def tables():
    k = np.arange(SIDE)[:, None]
    n = np.arange(SIDE)[None, :]
    rows = np.cos(np.pi * (2 * n + 1) * k / (2 * SIDE)) * np.sqrt(2.0 / SIDE)
    rows[0] *= np.sqrt(0.5)
    wide = np.kron(np.eye(2), rows).astype(np.float32)
    parts = []
    for a in (wide.T, wide):
        high = a.astype(bf16)
        parts += [high, (a - high.astype(np.float32)).astype(bf16)]
    parts.append(np.kron(np.eye(2), np.ones((SIDE, SIDE))).astype(bf16))
    return np.stack(parts)


def dot(a, b, dims=((1,), (0,))):
    return lax.dot_general(a, b, (dims, ((), ())), preferred_element_type=f32)


def dot3(a, b, dims=((1,), (0,))):
    return dot(a[0], b[0], dims) + (dot(a[0], b[1], dims) + dot(a[1], b[0], dims))


def one_hots(index_row):
    n = index_row.shape[1]
    lane = lax.broadcasted_iota(jnp.int32, (1, n), 1)
    row = index_row >> 6
    column = (index_row & 63) + jnp.where((lane & 63) >= 32, SIDE, 0)
    return (
        lax.broadcasted_iota(jnp.int32, (SIDE, n), 0) == row,
        lax.broadcasted_iota(jnp.int32, (PAIR, n), 0) == column,
    )


def cosines(index_row, table):
    row_hot, column_hot = (jnp.where(m, 1.0, 0.0).astype(bf16) for m in one_hots(index_row))
    rows = dot(table[WIDE_T, :SIDE, :SIDE], row_hot) + dot(table[WIDE_T + 1, :SIDE, :SIDE], row_hot)
    columns = dot(table[WIDE_T], column_hot) + dot(table[WIDE_T + 1], column_hot)
    return rows, columns


def index_line(indices):
    return jnp.concatenate([indices[b : b + 1, :] for b in range(indices.shape[0])], axis=1)


def split_hidden_kernel(place, hidden_far, after, mine, theirs, hidden, sems):
    even, c = place[0] == 0, place[1]
    copies = fetch(
        [hidden_far.at[:, pl.ds(zl * 1280, 1280)] for zl in range(4)],
        [hidden.at[:, pl.ds(zl * 1280, 1280)] for zl in range(4)],
        sems,
    )
    for zl in range(4):
        copies[zl].wait()
        for turn in range(2):
            core = c if turn == 0 else 1 - c
            both = hidden[:, pl.ds(pl.multiple_of(zl * 1280 + core * 640, 128), 640)]
            left, right = both[:, :320], both[:, 320:]
            start = turn * 1280 + zl * 320
            mine[:, start : start + 320] = jnp.where(even, left, right)
            theirs[:, start : start + 320] = jnp.where(even, right, left)


def fetch(sources, targets, sems):
    copies = [pltpu.make_async_copy(a, b, sems.at[i]) for i, (a, b) in enumerate(zip(sources, targets))]
    for copy in copies:
        copy.start()
    return copies


def values_kernel(momentum_far, gradient_far, indices_far, counts, table_far, sent, momentum, gradient, indices, table, sems):
    copies = fetch(
        (indices_far, table_far, momentum_far, gradient_far), (indices, table, momentum, gradient), sems
    )
    tiles = momentum.shape[1]
    copies[0].wait()
    copies[1].wait()
    line = index_line(indices)
    rows, columns = cosines(line, table)
    high, low = split(columns)
    lane = lax.broadcasted_iota(jnp.int32, (1, SIDE), 1)
    copies[2].wait()
    copies[3].wait()
    out = []
    for t in range(tiles):
        e = slice(t * SIDE, t * SIDE + SIDE)
        moment = decay_rate * momentum[0, t] + gradient[0, t].astype(f32)
        half = dot3(split(moment), (high[:, e], low[:, e]))
        value = jnp.sum(half * rows[:, e], axis=0, keepdims=True)
        live = (lane & 31) < jnp.where(lane < 32, counts[2 * t], counts[2 * t + 1])
        out.append(jnp.concatenate([jnp.where(live, value, 0.0), line[:, e].astype(f32)], axis=1))
    out.append(jnp.zeros((sent.shape[1] - tiles, PAIR), f32))
    out = jnp.concatenate(out, axis=0)
    for r in range(sent.shape[0]):
        sent[r] = out


def momentum_kernel(momentum_far, gradient_far, indices_far, sent, table_far, out, momentum, gradient, indices, table, sems):
    copies = fetch(
        (indices_far, table_far, momentum_far, gradient_far), (indices, table, momentum, gradient), sems
    )
    tiles = momentum.shape[1]
    for copy in copies:
        copy.wait()
    line = index_line(indices)
    rows, columns = cosines(line, table)
    high, low = split(columns)
    for t in range(tiles):
        e = slice(t * SIDE, t * SIDE + SIDE)
        moment = decay_rate * momentum[0, t] + gradient[0, t].astype(f32)
        weighted = rows[:, e] * sent[0, t : t + 1, :SIDE]
        out[0, t] = moment - dot3(split(weighted), (high[:, e], low[:, e]), ((1,), (1,)))


def update_kernel(place, got, weight_far, table_far, update, pieces, tanhs, weight, table, sems):
    copies = fetch((table_far, weight_far), (table, weight), sems)
    replicas, tiles = got.shape[0], weight.shape[0]
    values = jnp.concatenate([got[r, :, :SIDE] for r in range(replicas)], axis=1)
    indices = jnp.concatenate([got[r, :, SIDE:] for r in range(replicas)], axis=1).astype(jnp.int32)
    copies[0].wait()
    wide_t = table[WIDE_T, :SIDE, :SIDE], table[WIDE_T + 1, :SIDE, :SIDE]
    halves = []
    for t in range(tiles):
        row_hot, column_hot = one_hots(indices[t : t + 1, :])
        column_hot = jnp.where(column_hot, 1.0, 0.0).astype(bf16)
        weighted = split(jnp.where(row_hot, values[t : t + 1, :], 0.0))
        nt = ((1,), (1,))
        shared = (dot(weighted[0], column_hot, nt) + dot(weighted[1], column_hot, nt)) / replicas
        halves.append(dot3(wide_t, split(shared)))
    raw = dot3(split(jnp.concatenate(halves, axis=0)), (table[WIDE], table[WIDE + 1]))
    raw = raw.reshape(tiles, SIDE, PAIR)
    energy = jnp.sum(raw * raw, axis=1)
    e0, e1 = split(energy)
    energy = dot(e0, table[BLOCK_ONES]) + dot(e1, table[BLOCK_ONES])
    scale = jnp.sqrt(energy / (SIDE * SIDE) + tiny_eps)
    tanhs[...] = jnp.tanh(raw / scale[:, None, :])
    copies[1].wait()
    own_rows = pl.multiple_of(place[0] * 8, 8)
    for t in range(tiles):
        update[t] = tanhs[t, pl.ds(own_rows, 8), :].astype(bf16)
    first_tile = place[1] * (tiles // 2)
    first_row = pl.multiple_of(place[2] * 16, 16)
    for t in range(tiles // 2):
        moved = tanhs[first_tile + t, pl.ds(first_row, 16), :].astype(bf16).astype(f32)
        old = weight[first_tile + t, pl.ds(first_row, 16), :].astype(f32)
        new = (old - step_size * moved).astype(bf16)
        for z in range(pieces.shape[0]):
            pieces[z, t] = new


def fill(source, matrix):
    for z in range(16):
        for t in range(5):
            for y in range(4):
                row = z % 4 * 320 + t * 64 + y * 16
                matrix[row : row + 16, z // 4 * 128 : z // 4 * 128 + 128] = source[y, z, t]


def project_own_kernel(mine, xh_side, xl_side, across, weights, total, matrix):
    fill(weights, matrix)
    for s, tokens in enumerate((mine, xh_side, xl_side, across)):
        total[s] = jnp.dot(tokens[:, :HALF], matrix[...], preferred_element_type=f32)


def project_rest_kernel(place, mine, xh_side, xl_side, across, weights, total, out, matrix):
    fill(weights, matrix)
    for s, tokens in enumerate((mine, xh_side, xl_side, across)):
        part = jnp.dot(tokens[:, HALF:], matrix[...], preferred_element_type=f32)
        out[(place[0] ^ (s >> 1)) * 2 + (place[1] ^ (s & 1))] = (total[s] + part).astype(bf16)


def call(kernel, out_shape, *args, scratch=(), flops=0, moved=0, **more):
    return pl.pallas_call(
        kernel,
        out_shape=out_shape,
        scratch_shapes=list(scratch),
        compiler_params=pltpu.CompilerParams(vmem_limit_bytes=VMEM_LIMIT),
        cost_estimate=pl.CostEstimate(flops=flops, bytes_accessed=moved, transcendentals=0),
        **more,
    )(*args)


def shards(hidden, weight, momentum, gradient, indices, counts):
    tiles = weight.shape[0]
    table = jnp.asarray(tables())
    xl, y, xh, c = (lax.axis_index(a) for a in ("xl", "y", "xh", "c"))
    vm, sm, far = (pl.BlockSpec(memory_space=m) for m in (pltpu.VMEM, pltpu.SMEM, pltpu.HBM))
    shape = jax.ShapeDtypeStruct
    dmas = pltpu.SemaphoreType.DMA

    def scalars(*a):
        return jnp.stack(a).astype(jnp.int32)

    def room(*arrays):
        return [pltpu.VMEM(a.shape, a.dtype) for a in arrays]

    with jax.named_scope("own_values"):
        sent = call(
            values_kernel,
            shape((8, 16, PAIR), f32),
            momentum, gradient, indices[0], counts[0], table,
            scratch=room(momentum, gradient, indices[0], table) + [dmas((4,))],
            moved=2**19,
            in_specs=[far, far, far, sm, far],
            out_specs=vm,
        )

    with jax.named_scope("hidden_exchange"):
        mine, theirs = call(
            split_hidden_kernel,
            (shape((256, 2 * HALF), bf16),) * 2,
            scalars(xl, c), hidden, sent,
            scratch=room(hidden) + [dmas((4,))],
            moved=5 * 2**20,
            in_specs=[sm, far, far],
            out_specs=(vm, vm),
        )

    with jax.named_scope("replica_exchange"):
        got = lax.all_to_all(sent, ("xl", "y"), 0, 0)
        got, mine, theirs = lax.optimization_barrier((got, mine, theirs))

    with jax.named_scope("hidden_exchange"):
        swap, cross = [(0, 1), (1, 0)], [(0, 3), (1, 2), (2, 1), (3, 0)]
        xl_side = lax.ppermute(theirs, "xl", swap)
        across = lax.ppermute(theirs, ("xl", "xh"), cross)
        mine, xl_side, across = lax.optimization_barrier((mine, xl_side, across))
        xh_side = lax.ppermute(mine, "xh", swap)

    with jax.named_scope("new_weight"):
        update, pieces = call(
            update_kernel,
            (shape((tiles, 8, PAIR), bf16), shape((16, tiles // 2, 16, PAIR), bf16)),
            scalars(xl * 4 + y, xl, y), got, weight, table,
            scratch=[pltpu.VMEM((tiles, SIDE, PAIR), f32)] + room(weight, table) + [dmas((2,))],
            moved=2**19,
            in_specs=[sm, vm, far, far],
            out_specs=(vm, vm),
        )

    with jax.named_scope("weight_exchange"):
        along_z = lax.all_to_all(pieces, "z", 0, 0)
        along_y = lax.all_to_all(jnp.broadcast_to(along_z, (4,) + along_z.shape), "y", 0, 0)
        along_y, xh_side = lax.optimization_barrier((along_y, xh_side))
        other = lax.ppermute(along_y, "c", swap)

    with jax.named_scope("projection"):
        matrix = pltpu.VMEM((HALF, 512), bf16)
        total = call(
            project_own_kernel,
            shape((4, 256, 512), f32),
            mine, xh_side, xl_side, across, along_y,
            scratch=[matrix],
            flops=1024 * 2560 * 512, moved=2**20,
            in_specs=[vm] * 5,
            out_specs=vm,
        )
        partial = call(
            project_rest_kernel,
            shape((4, 256, 512), bf16),
            scalars(xl, xh), mine, xh_side, xl_side, across, other, total,
            scratch=[matrix],
            flops=1024 * 2560 * 512, moved=2**20,
            in_specs=[sm] + [vm] * 6,
            out_specs=vm,
        )

    with jax.named_scope("output_exchange"):
        back = lax.all_to_all(partial, ("xl", "xh"), 0, 0).astype(f32)
        back = back.reshape(2, 2, 256, 512).sum(0).astype(bf16)
        keys = jnp.concatenate([back[0], back[1]], axis=1)

    with jax.named_scope("momentum"):
        new_momentum = call(
            momentum_kernel,
            shape(momentum.shape, f32),
            momentum, gradient, indices[0], sent, table,
            scratch=room(momentum, gradient, indices[0], table) + [dmas((4,))],
            moved=2**20,
            in_specs=[far, far, far, vm, far],
            out_specs=vm,
        )
    return (keys, update, new_momentum)


def solution(mesh):
    fine = Mesh(mesh.devices.reshape(2, 4, 2, 16, 2), axes)
    rep, group = ("xl", "y"), ("xh", "z", "c")
    in_specs = (
        P(axes, None),
        P(group, None, None),
        P(rep, group, None, None),
        P(rep, group, None, None),
        P(rep, group, None),
        P(rep, group),
    )
    out_specs = (P(axes, None), P(group, rep, None), P(rep, group, None, None))
    return jax.shard_map(shards, mesh=fine, in_specs=in_specs, out_specs=out_specs, check_vma=False)
```

```python
import jax
import jax.numpy as jnp
import numpy as np
from jax import lax
from jax.experimental import pallas as pl
from jax.experimental.pallas import tpu as pltpu
from jax.sharding import Mesh, PartitionSpec as P

decay_rate = 0.999
step_size = 0.01
tiny_eps = 1e-06
SIDE = 64
PAIR = 128
f32 = jnp.float32
bf16 = jnp.bfloat16
axes = ("xl", "y", "xh", "z", "c")
VMEM_LIMIT = 16 * 2**20
MOST = 60 * 2**20
WIDE_T, WIDE, BLOCK_ONES = 0, 2, 4
HALF = 1280
OWN_FLOPS = 100 * 10**9
BAND = 64


def split(a):
    high = a.astype(bf16)
    return high, (a - high.astype(f32)).astype(bf16)


def tables():
    k = np.arange(SIDE)[:, None]
    n = np.arange(SIDE)[None, :]
    rows = np.cos(np.pi * (2 * n + 1) * k / (2 * SIDE)) * np.sqrt(2.0 / SIDE)
    rows[0] *= np.sqrt(0.5)
    wide = np.kron(np.eye(2), rows).astype(np.float32)
    parts = []
    for a in (wide.T, wide):
        high = a.astype(bf16)
        parts += [high, (a - high.astype(np.float32)).astype(bf16)]
    parts.append(np.kron(np.eye(2), np.ones((SIDE, SIDE))).astype(bf16))
    return np.stack(parts)


def dot(a, b, dims=((1,), (0,))):
    return lax.dot_general(a, b, (dims, ((), ())), preferred_element_type=f32)


def dot3(a, b, dims=((1,), (0,))):
    return dot(a[0], b[0], dims) + (dot(a[0], b[1], dims) + dot(a[1], b[0], dims))


def one_hots(index_row):
    n = index_row.shape[1]
    lane = lax.broadcasted_iota(jnp.int32, (1, n), 1)
    row = index_row >> 6
    column = (index_row & 63) + jnp.where((lane & 63) >= 32, SIDE, 0)
    return (
        lax.broadcasted_iota(jnp.int32, (SIDE, n), 0) == row,
        lax.broadcasted_iota(jnp.int32, (PAIR, n), 0) == column,
    )


def cosines(index_row, table):
    row_hot, column_hot = (jnp.where(m, 1.0, 0.0).astype(bf16) for m in one_hots(index_row))
    rows = dot(table[WIDE_T, :SIDE, :SIDE], row_hot) + dot(table[WIDE_T + 1, :SIDE, :SIDE], row_hot)
    columns = dot(table[WIDE_T], column_hot) + dot(table[WIDE_T + 1], column_hot)
    return rows, columns


def index_line(indices):
    return jnp.concatenate([indices[b] for b in range(indices.shape[0])], axis=1)


def split_hidden_kernel(hidden_far, after, mine_far, theirs_far, hidden, mine, theirs, sems):
    xl, c = lax.axis_index("xl"), lax.axis_index("c")
    bands = [pl.ds(i * BAND, BAND) for i in range(256 // BAND)]
    copies = fetch([hidden_far.at[k] for k in bands], [hidden.at[k] for k in bands], sems)
    left = lax.broadcasted_iota(jnp.int32, (BAND, 128), 1) < 64
    leaving = []
    for i, band in enumerate(bands):
        copies[i].wait()
        for turn in range(2):
            core = c if turn == 0 else 1 - c
            corners = []
            for zl in range(4):
                first = zl * 1280 + core * 640
                for out, half in ((theirs, 1 - xl), (mine, xl)):
                    start = turn * HALF + zl * 256
                    out[band, start : start + 256] = hidden[band, pl.ds(pl.multiple_of(first + half * 384, 128), 256)]
                corners.append(hidden[band, pl.ds(pl.multiple_of(first + 256, 128), 128)].astype(f32))
            for pair in range(2):
                a, b = corners[2 * pair : 2 * pair + 2]
                lows = jnp.where(left, a, pltpu.roll(b, 64, 1)).astype(bf16)
                highs = jnp.where(left, pltpu.roll(a, 64, 1), b).astype(bf16)
                start = turn * HALF + 1024 + pair * 128
                mine[band, start : start + 128] = jnp.where(xl == 0, lows, highs)
                theirs[band, start : start + 128] = jnp.where(xl == 0, highs, lows)
        leaving += fetch(
            (theirs.at[band], mine.at[band]),
            (theirs_far.at[band], mine_far.at[band]),
            [sems.at[len(bands) + 2 * i + j] for j in range(2)],
        )
    for copy in leaving:
        copy.wait()


def fetch(sources, targets, sems):
    sems = sems if isinstance(sems, list) else [sems.at[i] for i in range(len(sources))]
    copies = [pltpu.make_async_copy(*each) for each in zip(sources, targets, sems)]
    for copy in copies:
        copy.start()
    return copies


def values_kernel(momentum_far, gradient_far, indices_far, counts_far, table_far, sent, momentum, gradient, indices, counts, table, sems):
    copies = fetch(
        (indices_far, table_far, momentum_far, gradient_far, counts_far), (indices, table, momentum, gradient, counts), sems
    )
    tiles = momentum.shape[1]
    copies[0].wait()
    copies[1].wait()
    line = index_line(indices)
    rows, columns = cosines(line, table)
    high, low = split(columns)
    lane = lax.broadcasted_iota(jnp.int32, (1, SIDE), 1)
    for copy in copies[2:]:
        copy.wait()
    out = []
    for t in range(tiles):
        e = slice(t * SIDE, t * SIDE + SIDE)
        moment = decay_rate * momentum[0, t] + gradient[0, t].astype(f32)
        half = dot3(split(moment), (high[:, e], low[:, e]))
        value = jnp.sum(half * rows[:, e], axis=0, keepdims=True)
        live = (lane & 31) < jnp.where(lane < 32, counts[2 * t], counts[2 * t + 1])
        out.append(jnp.concatenate([jnp.where(live, value, 0.0), line[:, e].astype(f32)], axis=1))
    out.append(jnp.zeros((sent.shape[1] - tiles, PAIR), f32))
    out = jnp.concatenate(out, axis=0)
    for r in range(sent.shape[0]):
        sent[r] = out


def momentum_kernel(momentum, gradient, indices, sent, table, out):
    tiles = momentum.shape[1]
    line = index_line(indices)
    rows, columns = cosines(line, table)
    high, low = split(columns)
    for t in range(tiles):
        e = slice(t * SIDE, t * SIDE + SIDE)
        moment = decay_rate * momentum[0, t] + gradient[0, t].astype(f32)
        weighted = rows[:, e] * sent[0, t : t + 1, :SIDE]
        out[0, t] = moment - dot3(split(weighted), (high[:, e], low[:, e]), ((1,), (1,)))


def shared_directions(got, tiles, first_row, rows, table):
    replicas, nt = got.shape[0], ((1,), (1,))
    wide_t = [table[i, pl.ds(first_row, rows), :SIDE] for i in (WIDE_T, WIDE_T + 1)]
    halves, sums = [], []
    for t in tiles:
        lines = [got[r, pl.ds(t, 1), :] for r in range(replicas)]
        values = jnp.concatenate([line[:, :SIDE] for line in lines], axis=1)
        indices = jnp.concatenate([line[:, SIDE:] for line in lines], axis=1).astype(jnp.int32)
        row_hot, column_hot = one_hots(indices)
        column_hot = jnp.where(column_hot, 1.0, 0.0).astype(bf16)
        weighted = split(jnp.where(row_hot, values, 0.0))
        shared = (dot(weighted[0], column_hot, nt) + dot(weighted[1], column_hot, nt)) / replicas
        sums.append(jnp.sum(shared * shared, axis=0, keepdims=True))
        halves.append(dot3(wide_t, split(shared)))
    raw = dot3(split(jnp.concatenate(halves, axis=0)), (table[WIDE], table[WIDE + 1]))
    high, low = split(jnp.concatenate(sums, axis=0))
    energy = dot(high, table[BLOCK_ONES]) + dot(low, table[BLOCK_ONES])
    scale = jnp.sqrt(energy / (SIDE * SIDE) + tiny_eps)
    return jnp.tanh(raw.reshape(len(tiles), rows, PAIR) / scale[:, None, :])


def new_weight_kernel(got, weight, table, pieces):
    count = pieces.shape[1]
    first_tile = lax.axis_index("xl") * count
    first_row = pl.multiple_of(lax.axis_index("y") * 16, 16)
    tiles = [first_tile + t for t in range(count)]
    moved = shared_directions(got, tiles, first_row, 16, table).astype(bf16).astype(f32)
    for t in range(count):
        old = weight[tiles[t], pl.ds(first_row, 16), :].astype(f32)
        new = (old - step_size * moved[t]).astype(bf16)
        for z in range(pieces.shape[0]):
            pieces[z, t] = new


def update_kernel(got, table, update):
    first_row = pl.multiple_of((lax.axis_index("xl") * 4 + lax.axis_index("y")) * 8, 8)
    rows = pl.multiple_of(first_row // 16 * 16, 16)
    tanhs = shared_directions(got, list(range(update.shape[0])), rows, 16, table)
    upper = first_row == rows
    update[...] = jnp.where(upper, tanhs[:, :8], tanhs[:, 8:]).astype(bf16)


def fill_kernel(source, matrix):
    xl = lax.axis_index("xl")
    for z in range(16):
        for t in range(5):
            start = z % 4 * 256 + t * 64 if t < 4 else 1024 + z % 4 * 64
            tile = t + xl if t < 4 else 4 - 4 * xl
            for y in range(4):
                row = start + y * 16
                matrix[row : row + 16, z // 4 * 128 : z // 4 * 128 + 128] = source[y, z, tile]


def fetch_rows(tokens, start, rows, sems):
    return fetch([t.at[:, pl.ds(start, HALF)] for t in tokens], [rows.at[s] for s in range(4)], sems)


def project_own_kernel(mine, xh_side, xl_side, across, matrix, total, rows, sems):
    copies = fetch_rows((mine, xh_side, xl_side, across), 0, rows, sems)
    for s in range(4):
        copies[s].wait()
        total[s] = jnp.dot(rows[s], matrix[...], preferred_element_type=f32)


def project_rest_kernel(mine, xh_side, xl_side, across, matrix, total, out, rows, block, sems, out_sems):
    copies = fetch_rows((mine, xh_side, xl_side, across), HALF, rows, sems)
    xl, xh = lax.axis_index("xl"), lax.axis_index("xh")
    slots = xl * 2 + xh, xl * 2 + 1 - xh, (1 - xl) * 2 + xh, (1 - xl) * 2 + 1 - xh
    leaving = []
    for s in range(4):
        copies[s].wait()
        whole = total[s] + jnp.dot(rows[s], matrix[...], preferred_element_type=f32)
        block[s] = whole.astype(bf16)
        leaving += fetch([block.at[s]], [out.at[slots[s]]], [out_sems.at[s]])
    for copy in leaving:
        copy.wait()


def combine_kernel(back, keys):
    for xh in range(2):
        whole = back[xh].astype(f32) + back[2 + xh].astype(f32)
        keys[:, xh * 512 : xh * 512 + 512] = whole.astype(bf16)


def call(kernel, out_shape, *args, scratch=(), flops=0, moved=0, limit=VMEM_LIMIT, **more):
    return pl.pallas_call(
        kernel,
        out_shape=out_shape,
        scratch_shapes=list(scratch),
        compiler_params=pltpu.CompilerParams(vmem_limit_bytes=limit),
        cost_estimate=pl.CostEstimate(flops=flops, bytes_accessed=moved, transcendentals=0),
        **more,
    )(*args)


def shards(hidden, weight, momentum, gradient, indices, counts):
    tiles = weight.shape[0]
    table = jnp.asarray(tables())
    vm, far = (pl.BlockSpec(memory_space=m) for m in (pltpu.VMEM, pltpu.HBM))
    shape = jax.ShapeDtypeStruct
    dmas = pltpu.SemaphoreType.DMA

    def room(*arrays):
        return [pltpu.VMEM(a.shape, a.dtype) for a in arrays]

    lines = indices.reshape(2 * tiles, 1, indices.shape[2])
    with jax.named_scope("own_values"):
        sent = call(
            values_kernel,
            shape((8, 16, PAIR), f32),
            momentum, gradient, lines, counts[0], table,
            scratch=room(momentum, gradient, lines) + [pltpu.SMEM((2 * tiles,), jnp.int32)] + room(table) + [dmas((5,))],
            moved=2**19,
            limit=MOST,
            in_specs=[far] * 5,
            out_specs=vm,
        )

    with jax.named_scope("hidden_exchange"):
        mine, theirs = call(
            split_hidden_kernel,
            (shape((256, 2 * HALF), bf16),) * 2,
            hidden, sent,
            scratch=room(hidden) + [pltpu.VMEM((256, 2 * HALF), bf16)] * 2 + [dmas((12,))],
            moved=5 * 2**20,
            limit=MOST,
            in_specs=[far, pl.BlockSpec(memory_space=pl.ANY)],
            out_specs=(far, far),
        )

    with jax.named_scope("replica_exchange"):
        got = lax.all_to_all(sent, ("xl", "y"), 0, 0)
        got, mine, theirs = lax.optimization_barrier((got, mine, theirs))

    with jax.named_scope("hidden_exchange"):
        swap, cross = [(0, 1), (1, 0)], [(0, 3), (1, 2), (2, 1), (3, 0)]
        xh_side = lax.ppermute(mine, "xh", swap)
        theirs, xh_side = lax.optimization_barrier((theirs, xh_side))
        xl_side = lax.ppermute(theirs, "xl", swap)
        across = lax.ppermute(theirs, ("xl", "xh"), cross)

    with jax.named_scope("new_weight"):
        pieces = call(
            new_weight_kernel,
            shape((16, tiles // 2, 16, PAIR), bf16),
            got, weight, table,
            moved=2**19,
            in_specs=[vm] * 3,
            out_specs=vm,
        )
        update = call(
            update_kernel,
            shape((tiles, 8, PAIR), bf16),
            got, table,
            moved=2**19,
            in_specs=[vm] * 2,
            out_specs=vm,
        )

    with jax.named_scope("weight_exchange"):
        along_z = lax.all_to_all(pieces, "z", 0, 0)
        along_y = lax.all_to_all(jnp.broadcast_to(along_z, (4,) + along_z.shape), "y", 0, 0)
        matrix = shape((HALF, 512), bf16)
        own = call(fill_kernel, matrix, along_y, in_specs=[vm], out_specs=vm)
        other = lax.ppermute(own, "c", swap)

    with jax.named_scope("projection"):
        rows, anywhere = pltpu.VMEM((4, 256, HALF), bf16), pl.BlockSpec(memory_space=pl.ANY)
        total = call(
            project_own_kernel,
            shape((4, 256, 512), f32),
            mine, xh_side, xl_side, across, own,
            scratch=[rows, dmas((4,))],
            flops=OWN_FLOPS,
            in_specs=[anywhere] * 4 + [vm],
            out_specs=vm,
        )
        partial = call(
            project_rest_kernel,
            shape((4, 256, 512), bf16),
            mine, xh_side, xl_side, across, other, total,
            scratch=[rows, pltpu.VMEM((4, 256, 512), bf16), dmas((4,)), dmas((4,))],
            in_specs=[anywhere] * 4 + [vm, vm],
            out_specs=far,
        )

    with jax.named_scope("output_exchange"):
        back = lax.all_to_all(partial, ("xl", "xh"), 0, 0)
        keys = call(combine_kernel, shape((256, 1024), bf16), back, in_specs=[vm], out_specs=vm)

    with jax.named_scope("momentum"):
        new_momentum = call(
            momentum_kernel,
            shape(momentum.shape, f32),
            momentum, gradient, lines, sent, table,
            moved=2**20,
            in_specs=[vm] * 5,
            out_specs=vm,
        )
    return (keys, update, new_momentum)


def solution(mesh):
    fine = Mesh(mesh.devices.reshape(2, 4, 2, 16, 2), axes)
    rep, group = ("xl", "y"), ("xh", "z", "c")
    in_specs = (
        P(axes, None),
        P(group, None, None),
        P(rep, group, None, None),
        P(rep, group, None, None),
        P(rep, group, None),
        P(rep, group),
    )
    out_specs = (P(axes, None), P(group, rep, None), P(rep, group, None, None))
    return jax.shard_map(shards, mesh=fine, in_specs=in_specs, out_specs=out_specs, check_vma=False)
```

```python
import functools

import jax
import jax.numpy as jnp
import numpy as np
from jax import lax
from jax.experimental import pallas as pl
from jax.experimental.pallas import tpu as pltpu
from jax.sharding import Mesh, PartitionSpec as P

decay_rate = 0.999
step_size = 0.01
tiny_eps = 1e-06
SIDE = 64
PAIR = 128
f32 = jnp.float32
bf16 = jnp.bfloat16
axes = ("xl", "y", "xh", "z", "c")
VMEM_LIMIT = 16 * 2**20
MOST = 60 * 2**20
WIDE_T, WIDE, BLOCK_ONES = 0, 2, 4
HALF = 1280
OWN_FLOPS = 100 * 10**9


def split(a):
    high = a.astype(bf16)
    return high, (a - high.astype(f32)).astype(bf16)


def tables():
    k = np.arange(SIDE)[:, None]
    n = np.arange(SIDE)[None, :]
    rows = np.cos(np.pi * (2 * n + 1) * k / (2 * SIDE)) * np.sqrt(2.0 / SIDE)
    rows[0] *= np.sqrt(0.5)
    wide = np.kron(np.eye(2), rows).astype(np.float32)
    parts = []
    for a in (wide.T, wide):
        high = a.astype(bf16)
        parts += [high, (a - high.astype(np.float32)).astype(bf16)]
    parts.append(np.kron(np.eye(2), np.ones((SIDE, SIDE))).astype(bf16))
    return np.stack(parts)


def dot(a, b, dims=((1,), (0,))):
    return lax.dot_general(a, b, (dims, ((), ())), preferred_element_type=f32)


def dot3(a, b, dims=((1,), (0,))):
    return dot(a[0], b[0], dims) + (dot(a[0], b[1], dims) + dot(a[1], b[0], dims))


def one_hots(index_row):
    n = index_row.shape[1]
    lane = lax.broadcasted_iota(jnp.int32, (1, n), 1)
    row = index_row >> 6
    column = (index_row & 63) + jnp.where((lane & 63) >= 32, SIDE, 0)
    return (
        lax.broadcasted_iota(jnp.int32, (SIDE, n), 0) == row,
        lax.broadcasted_iota(jnp.int32, (PAIR, n), 0) == column,
    )


def cosines(index_row, table):
    row_hot, column_hot = (jnp.where(m, 1.0, 0.0).astype(bf16) for m in one_hots(index_row))
    rows = dot(table[WIDE_T, :SIDE, :SIDE], row_hot) + dot(table[WIDE_T + 1, :SIDE, :SIDE], row_hot)
    columns = dot(table[WIDE_T], column_hot) + dot(table[WIDE_T + 1], column_hot)
    return rows, columns


def index_line(indices):
    return jnp.concatenate([indices[b] for b in range(indices.shape[0])], axis=1)


def pack_hidden_kernel(keep, hidden_far, after, out_far, parts, out, sems):
    half = lax.axis_index("xl") if keep else 1 - lax.axis_index("xl")
    c = lax.axis_index("c")
    sources = []
    for turn in range(2):
        core = c if turn == 0 else 1 - c
        for zl in range(4):
            start = pl.multiple_of(zl * 1280 + core * 640 + half * 256, 128)
            sources.append(hidden_far.at[:, pl.ds(start, 384)])
    copies = fetch(sources, [parts.at[i] for i in range(8)], sems)
    left = lax.broadcasted_iota(jnp.int32, (256, 128), 1) < 64
    corner, body = pl.multiple_of(256 - half * 256, 128), pl.multiple_of(half * 128, 128)
    for turn in range(2):
        for zl in range(4):
            i = turn * 4 + zl
            copies[i].wait()
            start = turn * HALF + zl * 256
            out[:, start : start + 256] = parts[i, :, pl.ds(body, 256)]
            if zl % 2 == 1:
                a = parts[i - 1, :, pl.ds(corner, 128)].astype(f32)
                b = parts[i, :, pl.ds(corner, 128)].astype(f32)
                lows = jnp.where(left, a, pltpu.roll(b, 64, 1))
                highs = jnp.where(left, pltpu.roll(a, 64, 1), b)
                start = turn * HALF + 1024 + zl // 2 * 128
                out[:, start : start + 128] = jnp.where(half == 0, lows, highs).astype(bf16)
    bands = [pl.ds(i * 64, 64) for i in range(4)]
    for copy in fetch([out.at[k] for k in bands], [out_far.at[k] for k in bands], sems):
        copy.wait()


def fetch(sources, targets, sems):
    sems = sems if isinstance(sems, list) else [sems.at[i] for i in range(len(sources))]
    copies = [pltpu.make_async_copy(*each) for each in zip(sources, targets, sems)]
    for copy in copies:
        copy.start()
    return copies


def values_kernel(momentum_far, gradient_far, indices_far, counts_far, table_far, sent, momentum, gradient, indices, counts, table, sems):
    copies = fetch(
        (indices_far, table_far, momentum_far, gradient_far, counts_far), (indices, table, momentum, gradient, counts), sems
    )
    tiles = momentum.shape[1]
    copies[0].wait()
    copies[1].wait()
    line = index_line(indices)
    rows, columns = cosines(line, table)
    high, low = split(columns)
    lane = lax.broadcasted_iota(jnp.int32, (1, SIDE), 1)
    for copy in copies[2:]:
        copy.wait()
    out = []
    for t in range(tiles):
        e = slice(t * SIDE, t * SIDE + SIDE)
        moment = decay_rate * momentum[0, t] + gradient[0, t].astype(f32)
        half = dot3(split(moment), (high[:, e], low[:, e]))
        value = jnp.sum(half * rows[:, e], axis=0, keepdims=True)
        live = (lane & 31) < jnp.where(lane < 32, counts[2 * t], counts[2 * t + 1])
        out.append(jnp.concatenate([jnp.where(live, value, 0.0), line[:, e].astype(f32)], axis=1))
    out.append(jnp.zeros((sent.shape[1] - tiles, PAIR), f32))
    out = jnp.concatenate(out, axis=0)
    for r in range(sent.shape[0]):
        sent[r] = out


def momentum_kernel(momentum, gradient, indices, sent, table, out):
    tiles = momentum.shape[1]
    line = index_line(indices)
    rows, columns = cosines(line, table)
    high, low = split(columns)
    for t in range(tiles):
        e = slice(t * SIDE, t * SIDE + SIDE)
        moment = decay_rate * momentum[0, t] + gradient[0, t].astype(f32)
        weighted = rows[:, e] * sent[0, t : t + 1, :SIDE]
        out[0, t] = moment - dot3(split(weighted), (high[:, e], low[:, e]), ((1,), (1,)))


def shared_directions(got, tiles, first_row, rows, table):
    replicas, nt = got.shape[0], ((1,), (1,))
    wide_t = [table[i, pl.ds(first_row, rows), :SIDE] for i in (WIDE_T, WIDE_T + 1)]
    halves, sums = [], []
    for t in tiles:
        lines = [got[r, pl.ds(t, 1), :] for r in range(replicas)]
        values = jnp.concatenate([line[:, :SIDE] for line in lines], axis=1)
        indices = jnp.concatenate([line[:, SIDE:] for line in lines], axis=1).astype(jnp.int32)
        row_hot, column_hot = one_hots(indices)
        column_hot = jnp.where(column_hot, 1.0, 0.0).astype(bf16)
        weighted = split(jnp.where(row_hot, values, 0.0))
        shared = (dot(weighted[0], column_hot, nt) + dot(weighted[1], column_hot, nt)) / replicas
        sums.append(jnp.sum(shared * shared, axis=0, keepdims=True))
        halves.append(dot3(wide_t, split(shared)))
    raw = dot3(split(jnp.concatenate(halves, axis=0)), (table[WIDE], table[WIDE + 1]))
    high, low = split(jnp.concatenate(sums, axis=0))
    energy = dot(high, table[BLOCK_ONES]) + dot(low, table[BLOCK_ONES])
    scale = jnp.sqrt(energy / (SIDE * SIDE) + tiny_eps)
    return jnp.tanh(raw.reshape(len(tiles), rows, PAIR) / scale[:, None, :])


def new_weight_kernel(got, weight, table, pieces):
    count = pieces.shape[1]
    first_tile = lax.axis_index("xl") * count
    first_row = pl.multiple_of(lax.axis_index("y") * 16, 16)
    tiles = [first_tile + t for t in range(count)]
    moved = shared_directions(got, tiles, first_row, 16, table).astype(bf16).astype(f32)
    for t in range(count):
        old = weight[tiles[t], pl.ds(first_row, 16), :].astype(f32)
        new = (old - step_size * moved[t]).astype(bf16)
        for z in range(pieces.shape[0]):
            pieces[z, t] = new


def update_kernel(got, table, update):
    first_row = pl.multiple_of((lax.axis_index("xl") * 4 + lax.axis_index("y")) * 8, 8)
    rows = pl.multiple_of(first_row // 16 * 16, 16)
    tanhs = shared_directions(got, list(range(update.shape[0])), rows, 16, table)
    upper = first_row == rows
    update[...] = jnp.where(upper, tanhs[:, :8], tanhs[:, 8:]).astype(bf16)


def fill_kernel(source, matrix):
    xl = lax.axis_index("xl")
    for z in range(16):
        for t in range(5):
            start = z % 4 * 256 + t * 64 if t < 4 else 1024 + z % 4 * 64
            tile = t + xl if t < 4 else 4 - 4 * xl
            for y in range(4):
                row = start + y * 16
                matrix[row : row + 16, z // 4 * 128 : z // 4 * 128 + 128] = source[y, z, tile]


def fetch_rows(tokens, start, rows, sems):
    return fetch([t.at[:, pl.ds(start, HALF)] for t in tokens], [rows.at[s] for s in range(4)], sems)


def project_own_kernel(mine, xh_side, xl_side, across, matrix, total, rows, sems):
    copies = fetch_rows((mine, xh_side, xl_side, across), 0, rows, sems)
    for s in range(4):
        copies[s].wait()
        total[s] = jnp.dot(rows[s], matrix[...], preferred_element_type=f32)


def project_rest_kernel(mine, xh_side, xl_side, across, matrix, total, out, rows, block, sems, out_sems):
    copies = fetch_rows((mine, xh_side, xl_side, across), HALF, rows, sems)
    xl, xh = lax.axis_index("xl"), lax.axis_index("xh")
    slots = xl * 2 + xh, xl * 2 + 1 - xh, (1 - xl) * 2 + xh, (1 - xl) * 2 + 1 - xh
    leaving = []
    for s in range(4):
        copies[s].wait()
        whole = total[s] + jnp.dot(rows[s], matrix[...], preferred_element_type=f32)
        block[s] = whole.astype(bf16)
        leaving += fetch([block.at[s]], [out.at[slots[s]]], [out_sems.at[s]])
    for copy in leaving:
        copy.wait()


def combine_kernel(back, keys):
    for xh in range(2):
        whole = back[xh].astype(f32) + back[2 + xh].astype(f32)
        keys[:, xh * 512 : xh * 512 + 512] = whole.astype(bf16)


def call(kernel, out_shape, *args, scratch=(), flops=0, moved=0, limit=VMEM_LIMIT, **more):
    return pl.pallas_call(
        kernel,
        out_shape=out_shape,
        scratch_shapes=list(scratch),
        compiler_params=pltpu.CompilerParams(vmem_limit_bytes=limit),
        cost_estimate=pl.CostEstimate(flops=flops, bytes_accessed=moved, transcendentals=0),
        **more,
    )(*args)


def shards(hidden, weight, momentum, gradient, indices, counts):
    tiles = weight.shape[0]
    table = jnp.asarray(tables())
    vm, far = (pl.BlockSpec(memory_space=m) for m in (pltpu.VMEM, pltpu.HBM))
    shape = jax.ShapeDtypeStruct
    dmas = pltpu.SemaphoreType.DMA

    def room(*arrays):
        return [pltpu.VMEM(a.shape, a.dtype) for a in arrays]

    lines = indices.reshape(2 * tiles, 1, indices.shape[2])
    with jax.named_scope("own_values"):
        sent = call(
            values_kernel,
            shape((8, 16, PAIR), f32),
            momentum, gradient, lines, counts[0], table,
            scratch=room(momentum, gradient, lines) + [pltpu.SMEM((2 * tiles,), jnp.int32)] + room(table) + [dmas((5,))],
            moved=2**19,
            limit=MOST,
            in_specs=[far] * 5,
            out_specs=vm,
        )

    with jax.named_scope("hidden_exchange"):
        def pack(keep, after):
            return call(
                functools.partial(pack_hidden_kernel, keep),
                shape((256, 2 * HALF), bf16),
                hidden, after,
                scratch=[pltpu.VMEM((8, 256, 384), bf16), pltpu.VMEM((256, 2 * HALF), bf16), dmas((8,))],
                moved=2**22,
                limit=MOST,
                in_specs=[far, pl.BlockSpec(memory_space=pl.ANY)],
                out_specs=far,
            )

        mine = pack(True, sent)

    with jax.named_scope("replica_exchange"):
        got = lax.all_to_all(sent, ("xl", "y"), 0, 0)

    with jax.named_scope("hidden_exchange"):
        swap, cross = [(0, 1), (1, 0)], [(0, 3), (1, 2), (2, 1), (3, 0)]
        xh_side = lax.ppermute(mine, "xh", swap)
        theirs = pack(False, got)
        xl_side = lax.ppermute(theirs, "xl", swap)
        across = lax.ppermute(theirs, ("xl", "xh"), cross)

    with jax.named_scope("new_weight"):
        pieces = call(
            new_weight_kernel,
            shape((16, tiles // 2, 16, PAIR), bf16),
            got, weight, table,
            flops=OWN_FLOPS,
            in_specs=[vm] * 3,
            out_specs=vm,
        )
        update = call(
            update_kernel,
            shape((tiles, 8, PAIR), bf16),
            got, table,
            moved=2**19,
            in_specs=[vm] * 2,
            out_specs=vm,
        )

    with jax.named_scope("weight_exchange"):
        along_z = lax.all_to_all(pieces, "z", 0, 0)
        along_z, xh_side = lax.optimization_barrier((along_z, xh_side))
        along_y = lax.all_to_all(jnp.broadcast_to(along_z, (4,) + along_z.shape), "y", 0, 0)
        matrix = shape((HALF, 512), bf16)
        own = call(fill_kernel, matrix, along_y, in_specs=[vm], out_specs=vm)
        other = lax.ppermute(own, "c", swap)

    with jax.named_scope("projection"):
        rows, anywhere = pltpu.VMEM((4, 256, HALF), bf16), pl.BlockSpec(memory_space=pl.ANY)
        total = call(
            project_own_kernel,
            shape((4, 256, 512), f32),
            mine, xh_side, xl_side, across, own,
            scratch=[rows, dmas((4,))],
            flops=OWN_FLOPS,
            in_specs=[anywhere] * 4 + [vm],
            out_specs=vm,
        )
        partial = call(
            project_rest_kernel,
            shape((4, 256, 512), bf16),
            mine, xh_side, xl_side, across, other, total,
            scratch=[rows, pltpu.VMEM((4, 256, 512), bf16), dmas((4,)), dmas((4,))],
            in_specs=[anywhere] * 4 + [vm, vm],
            out_specs=far,
        )

    with jax.named_scope("output_exchange"):
        back = lax.all_to_all(partial, ("xl", "xh"), 0, 0)
        keys = call(combine_kernel, shape((256, 1024), bf16), back, in_specs=[vm], out_specs=vm)

    with jax.named_scope("momentum"):
        new_momentum = call(
            momentum_kernel,
            shape(momentum.shape, f32),
            momentum, gradient, lines, sent, table,
            moved=2**20,
            in_specs=[vm] * 5,
            out_specs=vm,
        )
    return (keys, update, new_momentum)


def solution(mesh):
    fine = Mesh(mesh.devices.reshape(2, 4, 2, 16, 2), axes)
    rep, group = ("xl", "y"), ("xh", "z", "c")
    in_specs = (
        P(axes, None),
        P(group, None, None),
        P(rep, group, None, None),
        P(rep, group, None, None),
        P(rep, group, None),
        P(rep, group),
    )
    out_specs = (P(axes, None), P(group, rep, None), P(rep, group, None, None))
    return jax.shard_map(shards, mesh=fine, in_specs=in_specs, out_specs=out_specs, check_vma=False)
```

```python
import jax
import jax.numpy as jnp
import numpy as np
from jax import lax
from jax.experimental import pallas as pl
from jax.experimental.pallas import tpu as pltpu
from jax.sharding import Mesh, PartitionSpec as P

decay_rate = 0.999
step_size = 0.01
tiny_eps = 1e-06
SIDE = 64
PAIR = 128
f32 = jnp.float32
bf16 = jnp.bfloat16
axes = ("xl", "y", "xh", "z", "c")
VMEM_LIMIT = 16 * 2**20
MOST = 60 * 2**20
WIDE_T, WIDE, BLOCK_ONES = 0, 2, 4
HALF = 1280
BAND = 64
OWN_FLOPS = 100 * 10**9


def split(a):
    high = a.astype(bf16)
    return high, (a - high.astype(f32)).astype(bf16)


def tables():
    k = np.arange(SIDE)[:, None]
    n = np.arange(SIDE)[None, :]
    rows = np.cos(np.pi * (2 * n + 1) * k / (2 * SIDE)) * np.sqrt(2.0 / SIDE)
    rows[0] *= np.sqrt(0.5)
    wide = np.kron(np.eye(2), rows).astype(np.float32)
    parts = []
    for a in (wide.T, wide):
        high = a.astype(bf16)
        parts += [high, (a - high.astype(np.float32)).astype(bf16)]
    parts.append(np.kron(np.eye(2), np.ones((SIDE, SIDE))).astype(bf16))
    return np.stack(parts)


def dot(a, b, dims=((1,), (0,))):
    return lax.dot_general(a, b, (dims, ((), ())), preferred_element_type=f32)


def dot3(a, b, dims=((1,), (0,))):
    return dot(a[0], b[0], dims) + (dot(a[0], b[1], dims) + dot(a[1], b[0], dims))


def one_hots(index_row):
    n = index_row.shape[1]
    lane = lax.broadcasted_iota(jnp.int32, (1, n), 1)
    row = index_row >> 6
    column = (index_row & 63) + jnp.where((lane & 63) >= 32, SIDE, 0)
    return (
        lax.broadcasted_iota(jnp.int32, (SIDE, n), 0) == row,
        lax.broadcasted_iota(jnp.int32, (PAIR, n), 0) == column,
    )


def cosines(index_row, table):
    row_hot, column_hot = (jnp.where(m, 1.0, 0.0).astype(bf16) for m in one_hots(index_row))
    rows = dot(table[WIDE_T, :SIDE, :SIDE], row_hot) + dot(table[WIDE_T + 1, :SIDE, :SIDE], row_hot)
    columns = dot(table[WIDE_T], column_hot) + dot(table[WIDE_T + 1], column_hot)
    return rows, columns


def index_line(indices):
    return jnp.concatenate([indices[b] for b in range(indices.shape[0])], axis=1)


def fetch(sources, targets, sems):
    sems = sems if isinstance(sems, list) else [sems.at[i] for i in range(len(sources))]
    copies = [pltpu.make_async_copy(*each) for each in zip(sources, targets, sems)]
    for copy in copies:
        copy.start()
    return copies


def start_hidden(hidden_far, hidden, sems):
    bands = [pl.ds(i * BAND, BAND) for i in range(256 // BAND)]
    return fetch([hidden_far.at[k] for k in bands], [hidden.at[k] for k in bands], sems)


def pack_hidden(half, copies, hidden, out, out_far, sems):
    c = lax.axis_index("c")
    left = lax.broadcasted_iota(jnp.int32, (BAND, 128), 1) < 64
    leaving = []
    for i, copy in enumerate(copies):
        copy.wait()
        band = pl.ds(i * BAND, BAND)
        for turn in range(2):
            core = c if turn == 0 else 1 - c
            corners = []
            for zl in range(4):
                first = zl * 1280 + core * 640
                start = turn * HALF + zl * 256
                out[band, start : start + 256] = hidden[band, pl.ds(pl.multiple_of(first + half * 384, 128), 256)]
                corners.append(hidden[band, pl.ds(pl.multiple_of(first + 256, 128), 128)].astype(f32))
            for pair in range(2):
                a, b = corners[2 * pair : 2 * pair + 2]
                lows = jnp.where(left, a, pltpu.roll(b, 64, 1))
                highs = jnp.where(left, pltpu.roll(a, 64, 1), b)
                start = turn * HALF + 1024 + pair * 128
                out[band, start : start + 128] = jnp.where(half == 0, lows, highs).astype(bf16)
        leaving += fetch([out.at[band]], [out_far.at[band]], [sems.at[len(copies) + i]])
    for copy in leaving:
        copy.wait()


def pack_theirs_kernel(hidden_far, after, out_far, parts, out, sems):
    half = 1 - lax.axis_index("xl")
    pack_hidden(half, start_hidden(hidden_far, parts, sems), parts, out, out_far, sems)


def values_kernel(
    momentum_far, gradient_far, indices_far, counts_far, table_far, hidden_far, sent, mine_far,
    momentum, gradient, indices, counts, table, parts, mine, sems, hidden_sems,
):
    copies = fetch(
        (indices_far, table_far, momentum_far, gradient_far, counts_far), (indices, table, momentum, gradient, counts), sems
    )
    half = lax.axis_index("xl")
    hidden_copies = start_hidden(hidden_far, parts, hidden_sems)
    tiles = momentum.shape[1]
    copies[0].wait()
    copies[1].wait()
    line = index_line(indices)
    rows, columns = cosines(line, table)
    high, low = split(columns)
    lane = lax.broadcasted_iota(jnp.int32, (1, SIDE), 1)
    for copy in copies[2:]:
        copy.wait()
    out = []
    for t in range(tiles):
        e = slice(t * SIDE, t * SIDE + SIDE)
        moment = decay_rate * momentum[0, t] + gradient[0, t].astype(f32)
        mixed = dot3(split(moment), (high[:, e], low[:, e]))
        value = jnp.sum(mixed * rows[:, e], axis=0, keepdims=True)
        live = (lane & 31) < jnp.where(lane < 32, counts[2 * t], counts[2 * t + 1])
        out.append(jnp.concatenate([jnp.where(live, value, 0.0), line[:, e].astype(f32)], axis=1))
    out.append(jnp.zeros((sent.shape[1] - tiles, PAIR), f32))
    out = jnp.concatenate(out, axis=0)
    for r in range(sent.shape[0]):
        sent[r] = out
    pack_hidden(half, hidden_copies, parts, mine, mine_far, hidden_sems)


def momentum_kernel(momentum, gradient, indices, sent, table, out):
    tiles = momentum.shape[1]
    line = index_line(indices)
    rows, columns = cosines(line, table)
    high, low = split(columns)
    for t in range(tiles):
        e = slice(t * SIDE, t * SIDE + SIDE)
        moment = decay_rate * momentum[0, t] + gradient[0, t].astype(f32)
        weighted = rows[:, e] * sent[0, t : t + 1, :SIDE]
        out[0, t] = moment - dot3(split(weighted), (high[:, e], low[:, e]), ((1,), (1,)))


def shared_directions(got, tiles, first_row, rows, table):
    replicas, nt = got.shape[0], ((1,), (1,))
    wide_t = [table[i, pl.ds(first_row, rows), :SIDE] for i in (WIDE_T, WIDE_T + 1)]
    halves, sums = [], []
    for t in tiles:
        lines = [got[r, pl.ds(t, 1), :] for r in range(replicas)]
        values = jnp.concatenate([line[:, :SIDE] for line in lines], axis=1)
        indices = jnp.concatenate([line[:, SIDE:] for line in lines], axis=1).astype(jnp.int32)
        row_hot, column_hot = one_hots(indices)
        column_hot = jnp.where(column_hot, 1.0, 0.0).astype(bf16)
        weighted = split(jnp.where(row_hot, values, 0.0))
        shared = (dot(weighted[0], column_hot, nt) + dot(weighted[1], column_hot, nt)) / replicas
        sums.append(jnp.sum(shared * shared, axis=0, keepdims=True))
        halves.append(dot3(wide_t, split(shared)))
    raw = dot3(split(jnp.concatenate(halves, axis=0)), (table[WIDE], table[WIDE + 1]))
    high, low = split(jnp.concatenate(sums, axis=0))
    energy = dot(high, table[BLOCK_ONES]) + dot(low, table[BLOCK_ONES])
    scale = jnp.sqrt(energy / (SIDE * SIDE) + tiny_eps)
    return jnp.tanh(raw.reshape(len(tiles), rows, PAIR) / scale[:, None, :])


def new_weight_kernel(got, weight, table, pieces):
    count = pieces.shape[1]
    first_tile = lax.axis_index("xl") * count
    first_row = pl.multiple_of(lax.axis_index("y") * 16, 16)
    tiles = [first_tile + t for t in range(count)]
    moved = shared_directions(got, tiles, first_row, 16, table).astype(bf16).astype(f32)
    for t in range(count):
        old = weight[tiles[t], pl.ds(first_row, 16), :].astype(f32)
        new = (old - step_size * moved[t]).astype(bf16)
        for z in range(pieces.shape[0]):
            pieces[z, t] = new


def update_kernel(got, table, update):
    first_row = pl.multiple_of((lax.axis_index("xl") * 4 + lax.axis_index("y")) * 8, 8)
    rows = pl.multiple_of(first_row // 16 * 16, 16)
    tanhs = shared_directions(got, list(range(update.shape[0])), rows, 16, table)
    upper = first_row == rows
    update[...] = jnp.where(upper, tanhs[:, :8], tanhs[:, 8:]).astype(bf16)


def fill_kernel(source, matrix):
    xl = lax.axis_index("xl")
    for z in range(16):
        for t in range(5):
            start = z % 4 * 256 + t * 64 if t < 4 else 1024 + z % 4 * 64
            tile = t + xl if t < 4 else 4 - 4 * xl
            for y in range(4):
                row = start + y * 16
                matrix[row : row + 16, z // 4 * 128 : z // 4 * 128 + 128] = source[y, z, tile]


def fetch_rows(tokens, start, rows, sems):
    return fetch([t.at[:, pl.ds(start, HALF)] for t in tokens], [rows.at[s] for s in range(4)], sems)


def project_own_kernel(mine, xh_side, xl_side, across, matrix, total, rows, sems):
    copies = fetch_rows((mine, xh_side, xl_side, across), 0, rows, sems)
    for s in range(4):
        copies[s].wait()
        total[s] = jnp.dot(rows[s], matrix[...], preferred_element_type=f32)


def project_rest_kernel(mine, xh_side, xl_side, across, matrix, total, out, rows, block, sems, out_sems):
    copies = fetch_rows((mine, xh_side, xl_side, across), HALF, rows, sems)
    xl, xh = lax.axis_index("xl"), lax.axis_index("xh")
    slots = xl * 2 + xh, xl * 2 + 1 - xh, (1 - xl) * 2 + xh, (1 - xl) * 2 + 1 - xh
    leaving = []
    for s in range(4):
        copies[s].wait()
        whole = total[s] + jnp.dot(rows[s], matrix[...], preferred_element_type=f32)
        block[s] = whole.astype(bf16)
        leaving += fetch([block.at[s]], [out.at[slots[s]]], [out_sems.at[s]])
    for copy in leaving:
        copy.wait()


def combine_kernel(back, keys):
    for xh in range(2):
        whole = back[xh].astype(f32) + back[2 + xh].astype(f32)
        keys[:, xh * 512 : xh * 512 + 512] = whole.astype(bf16)


def call(kernel, out_shape, *args, scratch=(), flops=0, moved=0, limit=VMEM_LIMIT, **more):
    return pl.pallas_call(
        kernel,
        out_shape=out_shape,
        scratch_shapes=list(scratch),
        compiler_params=pltpu.CompilerParams(vmem_limit_bytes=limit),
        cost_estimate=pl.CostEstimate(flops=flops, bytes_accessed=moved, transcendentals=0),
        **more,
    )(*args)


def shards(hidden, weight, momentum, gradient, indices, counts):
    tiles = weight.shape[0]
    table = jnp.asarray(tables())
    vm, far = (pl.BlockSpec(memory_space=m) for m in (pltpu.VMEM, pltpu.HBM))
    shape = jax.ShapeDtypeStruct
    dmas = pltpu.SemaphoreType.DMA

    def room(*arrays):
        return [pltpu.VMEM(a.shape, a.dtype) for a in arrays]

    lines = indices.reshape(2 * tiles, 1, indices.shape[2])
    with jax.named_scope("own_values"):
        packing = room(hidden) + [pltpu.VMEM((256, 2 * HALF), bf16)]
        sent, mine = call(
            values_kernel,
            (shape((8, 16, PAIR), f32), shape((256, 2 * HALF), bf16)),
            momentum, gradient, lines, counts[0], table, hidden,
            scratch=room(momentum, gradient, lines) + [pltpu.SMEM((2 * tiles,), jnp.int32)] + room(table) + packing + [dmas((5,)), dmas((8,))],
            moved=2**19,
            limit=MOST,
            in_specs=[far] * 6,
            out_specs=(vm, far),
        )

    with jax.named_scope("replica_exchange"):
        got = lax.all_to_all(sent, ("xl", "y"), 0, 0)

    with jax.named_scope("hidden_exchange"):
        swap, cross = [(0, 1), (1, 0)], [(0, 3), (1, 2), (2, 1), (3, 0)]
        xh_side = lax.ppermute(mine, "xh", swap)
        theirs = call(
            pack_theirs_kernel,
            shape((256, 2 * HALF), bf16),
            hidden, got,
            scratch=packing + [dmas((8,))],
            moved=2**22,
            limit=MOST,
            in_specs=[far, pl.BlockSpec(memory_space=pl.ANY)],
            out_specs=far,
        )
        xl_side = lax.ppermute(theirs, "xl", swap)
        across = lax.ppermute(theirs, ("xl", "xh"), cross)

    with jax.named_scope("new_weight"):
        pieces = call(
            new_weight_kernel,
            shape((16, tiles // 2, 16, PAIR), bf16),
            got, weight, table,
            flops=OWN_FLOPS,
            in_specs=[vm] * 3,
            out_specs=vm,
        )
        update = call(
            update_kernel,
            shape((tiles, 8, PAIR), bf16),
            got, table,
            moved=2**19,
            in_specs=[vm] * 2,
            out_specs=vm,
        )

    with jax.named_scope("weight_exchange"):
        along_z = lax.all_to_all(pieces, "z", 0, 0)
        along_z, xh_side = lax.optimization_barrier((along_z, xh_side))
        along_y = lax.all_to_all(jnp.broadcast_to(along_z, (4,) + along_z.shape), "y", 0, 0)
        matrix = shape((HALF, 512), bf16)
        own = call(fill_kernel, matrix, along_y, in_specs=[vm], out_specs=vm)
        other = lax.ppermute(own, "c", swap)

    with jax.named_scope("projection"):
        rows, anywhere = pltpu.VMEM((4, 256, HALF), bf16), pl.BlockSpec(memory_space=pl.ANY)
        total = call(
            project_own_kernel,
            shape((4, 256, 512), f32),
            mine, xh_side, xl_side, across, own,
            scratch=[rows, dmas((4,))],
            flops=OWN_FLOPS,
            in_specs=[anywhere] * 4 + [vm],
            out_specs=vm,
        )
        partial = call(
            project_rest_kernel,
            shape((4, 256, 512), bf16),
            mine, xh_side, xl_side, across, other, total,
            scratch=[rows, pltpu.VMEM((4, 256, 512), bf16), dmas((4,)), dmas((4,))],
            in_specs=[anywhere] * 4 + [vm, vm],
            out_specs=far,
        )

    with jax.named_scope("output_exchange"):
        back = lax.all_to_all(partial, ("xl", "xh"), 0, 0)
        keys = call(combine_kernel, shape((256, 1024), bf16), back, in_specs=[vm], out_specs=vm)

    with jax.named_scope("momentum"):
        new_momentum = call(
            momentum_kernel,
            shape(momentum.shape, f32),
            momentum, gradient, lines, sent, table,
            moved=2**20,
            in_specs=[vm] * 5,
            out_specs=vm,
        )
    return (keys, update, new_momentum)


def solution(mesh):
    fine = Mesh(mesh.devices.reshape(2, 4, 2, 16, 2), axes)
    rep, group = ("xl", "y"), ("xh", "z", "c")
    in_specs = (
        P(axes, None),
        P(group, None, None),
        P(rep, group, None, None),
        P(rep, group, None, None),
        P(rep, group, None),
        P(rep, group),
    )
    out_specs = (P(axes, None), P(group, rep, None), P(rep, group, None, None))
    return jax.shard_map(shards, mesh=fine, in_specs=in_specs, out_specs=out_specs, check_vma=False)
```

```python
import jax
import jax.numpy as jnp
import numpy as np
from jax import lax
from jax.experimental import pallas as pl
from jax.experimental.pallas import tpu as pltpu
from jax.sharding import Mesh, PartitionSpec as P

decay_rate = 0.999
step_size = 0.01
tiny_eps = 1e-06
SIDE = 64
PAIR = 128
f32 = jnp.float32
bf16 = jnp.bfloat16
axes = ("xl", "y", "xh", "z", "c")
VMEM_LIMIT = 16 * 2**20
MOST = 60 * 2**20
WIDE_T, WIDE, BLOCK_ONES = 0, 2, 4
HALF = 1280
BAND = 64
OWN_FLOPS = 100 * 10**9


def split(a):
    high = a.astype(bf16)
    return high, (a - high.astype(f32)).astype(bf16)


def tables():
    k = np.arange(SIDE)[:, None]
    n = np.arange(SIDE)[None, :]
    rows = np.cos(np.pi * (2 * n + 1) * k / (2 * SIDE)) * np.sqrt(2.0 / SIDE)
    rows[0] *= np.sqrt(0.5)
    wide = np.kron(np.eye(2), rows).astype(np.float32)
    parts = []
    for a in (wide.T, wide):
        high = a.astype(bf16)
        parts += [high, (a - high.astype(np.float32)).astype(bf16)]
    parts.append(np.kron(np.eye(2), np.ones((SIDE, SIDE))).astype(bf16))
    return np.stack(parts)


def dot(a, b, dims=((1,), (0,))):
    return lax.dot_general(a, b, (dims, ((), ())), preferred_element_type=f32)


def dot3(a, b, dims=((1,), (0,))):
    return dot(a[0], b[0], dims) + (dot(a[0], b[1], dims) + dot(a[1], b[0], dims))


def one_hots(index_row):
    n = index_row.shape[1]
    lane = lax.broadcasted_iota(jnp.int32, (1, n), 1)
    row = index_row >> 6
    column = (index_row & 63) + jnp.where((lane & 63) >= 32, SIDE, 0)
    return (
        lax.broadcasted_iota(jnp.int32, (SIDE, n), 0) == row,
        lax.broadcasted_iota(jnp.int32, (PAIR, n), 0) == column,
    )


def cosines(index_row, table):
    row_hot, column_hot = (jnp.where(m, 1.0, 0.0).astype(bf16) for m in one_hots(index_row))
    rows = dot(table[WIDE_T, :SIDE, :SIDE], row_hot) + dot(table[WIDE_T + 1, :SIDE, :SIDE], row_hot)
    columns = dot(table[WIDE_T], column_hot) + dot(table[WIDE_T + 1], column_hot)
    return rows, columns


def index_line(indices):
    return jnp.concatenate([indices[b] for b in range(indices.shape[0])], axis=1)


def fetch(sources, targets, sems):
    sems = sems if isinstance(sems, list) else [sems.at[i] for i in range(len(sources))]
    copies = [pltpu.make_async_copy(*each) for each in zip(sources, targets, sems)]
    for copy in copies:
        copy.start()
    return copies


def start_hidden(hidden_far, hidden, sems):
    bands = [pl.ds(i * BAND, BAND) for i in range(256 // BAND)]
    return fetch([hidden_far.at[k] for k in bands], [hidden.at[k] for k in bands], sems)


def pack_hidden(half, copies, hidden, out, out_far, sems):
    c = lax.axis_index("c")
    left = lax.broadcasted_iota(jnp.int32, (BAND, 128), 1) < 64
    leaving = []
    for i, copy in enumerate(copies):
        copy.wait()
        band = pl.ds(i * BAND, BAND)
        for turn in range(2):
            core = c if turn == 0 else 1 - c
            corners = []
            for zl in range(4):
                first = zl * 1280 + core * 640
                start = turn * HALF + zl * 256
                out[band, start : start + 256] = hidden[band, pl.ds(pl.multiple_of(first + half * 384, 128), 256)]
                corners.append(hidden[band, pl.ds(pl.multiple_of(first + 256, 128), 128)].astype(f32))
            for pair in range(2):
                a, b = corners[2 * pair : 2 * pair + 2]
                lows = jnp.where(left, a, pltpu.roll(b, 64, 1))
                highs = jnp.where(left, pltpu.roll(a, 64, 1), b)
                start = turn * HALF + 1024 + pair * 128
                out[band, start : start + 128] = jnp.where(half == 0, lows, highs).astype(bf16)
        leaving += fetch([out.at[band]], [out_far.at[band]], [sems.at[len(copies) + i]])
    for copy in leaving:
        copy.wait()


def pack_theirs_kernel(hidden_far, after, out_far, parts, out, sems):
    half = 1 - lax.axis_index("xl")
    pack_hidden(half, start_hidden(hidden_far, parts, sems), parts, out, out_far, sems)


def values_kernel(
    momentum_far, gradient_far, indices_far, counts_far, table_far, hidden_far, sent, mine_far,
    momentum, gradient, indices, counts, table, parts, mine, sems, hidden_sems,
):
    copies = fetch(
        (indices_far, table_far, momentum_far, gradient_far, counts_far), (indices, table, momentum, gradient, counts), sems
    )
    half = lax.axis_index("xl")
    hidden_copies = start_hidden(hidden_far, parts, hidden_sems)
    tiles = momentum.shape[1]
    copies[0].wait()
    copies[1].wait()
    line = index_line(indices)
    rows, columns = cosines(line, table)
    high, low = split(columns)
    lane = lax.broadcasted_iota(jnp.int32, (1, SIDE), 1)
    for copy in copies[2:]:
        copy.wait()
    out = []
    for t in range(tiles):
        e = slice(t * SIDE, t * SIDE + SIDE)
        moment = decay_rate * momentum[0, t] + gradient[0, t].astype(f32)
        mixed = dot3(split(moment), (high[:, e], low[:, e]))
        value = jnp.sum(mixed * rows[:, e], axis=0, keepdims=True)
        live = (lane & 31) < jnp.where(lane < 32, counts[2 * t], counts[2 * t + 1])
        out.append(jnp.concatenate([jnp.where(live, value, 0.0), line[:, e].astype(f32)], axis=1))
    out.append(jnp.zeros((sent.shape[1] - tiles, PAIR), f32))
    out = jnp.concatenate(out, axis=0)
    for r in range(sent.shape[0]):
        sent[r] = out
    pack_hidden(half, hidden_copies, parts, mine, mine_far, hidden_sems)


def momentum_kernel(momentum, gradient, indices, sent, table, out):
    tiles = momentum.shape[1]
    line = index_line(indices)
    rows, columns = cosines(line, table)
    high, low = split(columns)
    for t in range(tiles):
        e = slice(t * SIDE, t * SIDE + SIDE)
        moment = decay_rate * momentum[0, t] + gradient[0, t].astype(f32)
        weighted = rows[:, e] * sent[0, t : t + 1, :SIDE]
        out[0, t] = moment - dot3(split(weighted), (high[:, e], low[:, e]), ((1,), (1,)))


def shared_directions(got, tiles, first_row, rows, table):
    replicas, nt = got.shape[0], ((1,), (1,))
    wide_t = [table[i, pl.ds(first_row, rows), :SIDE] for i in (WIDE_T, WIDE_T + 1)]
    halves, sums = [], []
    for t in tiles:
        lines = [got[r, pl.ds(t, 1), :] for r in range(replicas)]
        values = jnp.concatenate([line[:, :SIDE] for line in lines], axis=1)
        indices = jnp.concatenate([line[:, SIDE:] for line in lines], axis=1).astype(jnp.int32)
        row_hot, column_hot = one_hots(indices)
        column_hot = jnp.where(column_hot, 1.0, 0.0).astype(bf16)
        weighted = split(jnp.where(row_hot, values, 0.0))
        shared = (dot(weighted[0], column_hot, nt) + dot(weighted[1], column_hot, nt)) / replicas
        sums.append(jnp.sum(shared * shared, axis=0, keepdims=True))
        halves.append(dot3(wide_t, split(shared)))
    raw = dot3(split(jnp.concatenate(halves, axis=0)), (table[WIDE], table[WIDE + 1]))
    high, low = split(jnp.concatenate(sums, axis=0))
    energy = dot(high, table[BLOCK_ONES]) + dot(low, table[BLOCK_ONES])
    scale = jnp.sqrt(energy / (SIDE * SIDE) + tiny_eps)
    return jnp.tanh(raw.reshape(len(tiles), rows, PAIR) / scale[:, None, :])


def new_weight_kernel(got, weight, table, pieces):
    count = pieces.shape[1]
    first_tile = lax.axis_index("xl") * count
    first_row = pl.multiple_of(lax.axis_index("y") * 16, 16)
    tiles = [first_tile + t for t in range(count)]
    moved = shared_directions(got, tiles, first_row, 16, table).astype(bf16).astype(f32)
    for t in range(count):
        old = weight[tiles[t], pl.ds(first_row, 16), :].astype(f32)
        new = (old - step_size * moved[t]).astype(bf16)
        for z in range(pieces.shape[0]):
            pieces[z, t] = new


def update_kernel(got, table, update):
    first_row = pl.multiple_of((lax.axis_index("xl") * 4 + lax.axis_index("y")) * 8, 8)
    rows = pl.multiple_of(first_row // 16 * 16, 16)
    tanhs = shared_directions(got, list(range(update.shape[0])), rows, 16, table)
    upper = first_row == rows
    update[...] = jnp.where(upper, tanhs[:, :8], tanhs[:, 8:]).astype(bf16)


def fill_kernel(source, matrix):
    xl = lax.axis_index("xl")
    for z in range(16):
        for t in range(5):
            start = z % 4 * 256 + t * 64 if t < 4 else 1024 + z % 4 * 64
            tile = t + xl if t < 4 else 4 - 4 * xl
            for y in range(4):
                row = start + y * 16
                matrix[row : row + 16, z // 4 * 128 : z // 4 * 128 + 128] = source[y, z, tile]


def fetch_rows(tokens, start, rows, sems):
    return fetch([t.at[:, pl.ds(start, HALF)] for t in tokens], [rows.at[s] for s in range(4)], sems)


def project_own_kernel(mine, xh_side, xl_side, across, matrix, total, later, rows, sems):
    tokens = mine, xh_side, xl_side, across
    copies = fetch_rows(tokens, 0, rows, sems)
    rest = fetch_rows(tokens, HALF, later, [sems.at[4 + s] for s in range(4)])
    for s in range(4):
        copies[s].wait()
        total[s] = jnp.dot(rows[s], matrix[...], preferred_element_type=f32)
    for copy in rest:
        copy.wait()


def project_rest_kernel(rows, matrix, total, out, block, out_sems):
    xl, xh = lax.axis_index("xl"), lax.axis_index("xh")
    slots = xl * 2 + xh, xl * 2 + 1 - xh, (1 - xl) * 2 + xh, (1 - xl) * 2 + 1 - xh
    leaving = []
    for s in range(4):
        whole = total[s] + jnp.dot(rows[s], matrix[...], preferred_element_type=f32)
        block[s] = whole.astype(bf16)
        leaving += fetch([block.at[s]], [out.at[slots[s]]], [out_sems.at[s]])
    for copy in leaving:
        copy.wait()


def combine_kernel(back, keys):
    for xh in range(2):
        whole = back[xh].astype(f32) + back[2 + xh].astype(f32)
        keys[:, xh * 512 : xh * 512 + 512] = whole.astype(bf16)


def call(kernel, out_shape, *args, scratch=(), flops=0, moved=0, limit=VMEM_LIMIT, **more):
    return pl.pallas_call(
        kernel,
        out_shape=out_shape,
        scratch_shapes=list(scratch),
        compiler_params=pltpu.CompilerParams(vmem_limit_bytes=limit),
        cost_estimate=pl.CostEstimate(flops=flops, bytes_accessed=moved, transcendentals=0),
        **more,
    )(*args)


def shards(hidden, weight, momentum, gradient, indices, counts):
    tiles = weight.shape[0]
    table = jnp.asarray(tables())
    vm, far = (pl.BlockSpec(memory_space=m) for m in (pltpu.VMEM, pltpu.HBM))
    shape = jax.ShapeDtypeStruct
    dmas = pltpu.SemaphoreType.DMA

    def room(*arrays):
        return [pltpu.VMEM(a.shape, a.dtype) for a in arrays]

    lines = indices.reshape(2 * tiles, 1, indices.shape[2])
    with jax.named_scope("own_values"):
        packing = room(hidden) + [pltpu.VMEM((256, 2 * HALF), bf16)]
        sent, mine = call(
            values_kernel,
            (shape((8, 16, PAIR), f32), shape((256, 2 * HALF), bf16)),
            momentum, gradient, lines, counts[0], table, hidden,
            scratch=room(momentum, gradient, lines) + [pltpu.SMEM((2 * tiles,), jnp.int32)] + room(table) + packing + [dmas((5,)), dmas((8,))],
            moved=2**19,
            limit=MOST,
            in_specs=[far] * 6,
            out_specs=(vm, far),
        )

    with jax.named_scope("replica_exchange"):
        got = lax.all_to_all(sent, ("xl", "y"), 0, 0)

    with jax.named_scope("hidden_exchange"):
        swap, cross = [(0, 1), (1, 0)], [(0, 3), (1, 2), (2, 1), (3, 0)]
        xh_side = lax.ppermute(mine, "xh", swap)
        theirs = call(
            pack_theirs_kernel,
            shape((256, 2 * HALF), bf16),
            hidden, got,
            scratch=packing + [dmas((8,))],
            moved=2**22,
            limit=MOST,
            in_specs=[far, pl.BlockSpec(memory_space=pl.ANY)],
            out_specs=far,
        )
        xl_side = lax.ppermute(theirs, "xl", swap)
        across = lax.ppermute(theirs, ("xl", "xh"), cross)

    with jax.named_scope("new_weight"):
        pieces = call(
            new_weight_kernel,
            shape((16, tiles // 2, 16, PAIR), bf16),
            got, weight, table,
            flops=OWN_FLOPS,
            in_specs=[vm] * 3,
            out_specs=vm,
        )
        update = call(
            update_kernel,
            shape((tiles, 8, PAIR), bf16),
            got, table,
            moved=2**19,
            in_specs=[vm] * 2,
            out_specs=vm,
        )

    with jax.named_scope("weight_exchange"):
        along_z = lax.all_to_all(pieces, "z", 0, 0)
        along_z, xh_side = lax.optimization_barrier((along_z, xh_side))
        along_y = lax.all_to_all(jnp.broadcast_to(along_z, (4,) + along_z.shape), "y", 0, 0)
        matrix = shape((HALF, 512), bf16)
        own = call(fill_kernel, matrix, along_y, in_specs=[vm], out_specs=vm)
        other = lax.ppermute(own, "c", swap)

    with jax.named_scope("projection"):
        anywhere, half_rows = pl.BlockSpec(memory_space=pl.ANY), (4, 256, HALF)
        total, later = call(
            project_own_kernel,
            (shape((4, 256, 512), f32), shape(half_rows, bf16)),
            mine, xh_side, xl_side, across, own,
            scratch=[pltpu.VMEM(half_rows, bf16), dmas((8,))],
            flops=OWN_FLOPS,
            in_specs=[anywhere] * 4 + [vm],
            out_specs=(vm, vm),
        )
        partial = call(
            project_rest_kernel,
            shape((4, 256, 512), bf16),
            later, other, total,
            scratch=[pltpu.VMEM((4, 256, 512), bf16), dmas((4,))],
            in_specs=[vm] * 3,
            out_specs=far,
        )

    with jax.named_scope("output_exchange"):
        back = lax.all_to_all(partial, ("xl", "xh"), 0, 0)
        keys = call(combine_kernel, shape((256, 1024), bf16), back, in_specs=[vm], out_specs=vm)

    with jax.named_scope("momentum"):
        new_momentum = call(
            momentum_kernel,
            shape(momentum.shape, f32),
            momentum, gradient, lines, sent, table,
            moved=2**20,
            in_specs=[vm] * 5,
            out_specs=vm,
        )
    return (keys, update, new_momentum)


def solution(mesh):
    fine = Mesh(mesh.devices.reshape(2, 4, 2, 16, 2), axes)
    rep, group = ("xl", "y"), ("xh", "z", "c")
    in_specs = (
        P(axes, None),
        P(group, None, None),
        P(rep, group, None, None),
        P(rep, group, None, None),
        P(rep, group, None),
        P(rep, group),
    )
    out_specs = (P(axes, None), P(group, rep, None), P(rep, group, None, None))
    return jax.shard_map(shards, mesh=fine, in_specs=in_specs, out_specs=out_specs, check_vma=False)
```

```python
import jax
import jax.numpy as jnp
import numpy as np
from jax import lax
from jax.experimental import pallas as pl
from jax.experimental.pallas import tpu as pltpu
from jax.sharding import Mesh, PartitionSpec as P

decay_rate = 0.999
step_size = 0.01
tiny_eps = 1e-06
SIDE = 64
PAIR = 128
f32 = jnp.float32
bf16 = jnp.bfloat16
axes = ("xl", "y", "xh", "z", "c")
VMEM_LIMIT = 16 * 2**20
MOST = 60 * 2**20
WIDE_T, WIDE, BLOCK_ONES = 0, 2, 4
HALF = 1280
BAND = 64
OWN_FLOPS = 100 * 10**9


def split(a):
    high = a.astype(bf16)
    return high, (a - high.astype(f32)).astype(bf16)


def tables():
    k = np.arange(SIDE)[:, None]
    n = np.arange(SIDE)[None, :]
    rows = np.cos(np.pi * (2 * n + 1) * k / (2 * SIDE)) * np.sqrt(2.0 / SIDE)
    rows[0] *= np.sqrt(0.5)
    wide = np.kron(np.eye(2), rows).astype(np.float32)
    parts = []
    for a in (wide.T, wide):
        high = a.astype(bf16)
        parts += [high, (a - high.astype(np.float32)).astype(bf16)]
    parts.append(np.kron(np.eye(2), np.ones((SIDE, SIDE))).astype(bf16))
    return np.stack(parts)


def dot(a, b, dims=((1,), (0,))):
    return lax.dot_general(a, b, (dims, ((), ())), preferred_element_type=f32)


def dot3(a, b, dims=((1,), (0,))):
    return dot(a[0], b[0], dims) + (dot(a[0], b[1], dims) + dot(a[1], b[0], dims))


def one_hots(index_row):
    n = index_row.shape[1]
    lane = lax.broadcasted_iota(jnp.int32, (1, n), 1)
    row = index_row >> 6
    column = (index_row & 63) + jnp.where((lane & 63) >= 32, SIDE, 0)
    return (
        lax.broadcasted_iota(jnp.int32, (SIDE, n), 0) == row,
        lax.broadcasted_iota(jnp.int32, (PAIR, n), 0) == column,
    )


def cosines(index_row, table):
    row_hot, column_hot = (jnp.where(m, 1.0, 0.0).astype(bf16) for m in one_hots(index_row))
    rows = dot(table[WIDE_T, :SIDE, :SIDE], row_hot) + dot(table[WIDE_T + 1, :SIDE, :SIDE], row_hot)
    columns = dot(table[WIDE_T], column_hot) + dot(table[WIDE_T + 1], column_hot)
    return rows, columns


def index_line(indices):
    return jnp.concatenate([indices[b] for b in range(indices.shape[0])], axis=1)


def fetch(sources, targets, sems):
    sems = sems if isinstance(sems, list) else [sems.at[i] for i in range(len(sources))]
    copies = [pltpu.make_async_copy(*each) for each in zip(sources, targets, sems)]
    for copy in copies:
        copy.start()
    return copies


def start_hidden(hidden_far, hidden, sems):
    bands = [pl.ds(i * BAND, BAND) for i in range(256 // BAND)]
    return fetch([hidden_far.at[k] for k in bands], [hidden.at[k] for k in bands], sems)


def pack_hidden(half, copies, hidden, out, out_far, sems):
    c = lax.axis_index("c")
    left = lax.broadcasted_iota(jnp.int32, (BAND, 128), 1) < 64
    leaving = []
    for i, copy in enumerate(copies):
        copy.wait()
        band = pl.ds(i * BAND, BAND)
        for turn in range(2):
            core = c if turn == 0 else 1 - c
            corners = []
            for zl in range(4):
                first = zl * 1280 + core * 640
                start = turn * HALF + zl * 256
                out[band, start : start + 256] = hidden[band, pl.ds(pl.multiple_of(first + half * 384, 128), 256)]
                corners.append(hidden[band, pl.ds(pl.multiple_of(first + 256, 128), 128)].astype(f32))
            for pair in range(2):
                a, b = corners[2 * pair : 2 * pair + 2]
                lows = jnp.where(left, a, pltpu.roll(b, 64, 1))
                highs = jnp.where(left, pltpu.roll(a, 64, 1), b)
                start = turn * HALF + 1024 + pair * 128
                out[band, start : start + 128] = jnp.where(half == 0, lows, highs).astype(bf16)
        leaving += fetch([out.at[band]], [out_far.at[band]], [sems.at[len(copies) + i]])
    for copy in leaving:
        copy.wait()


def pack_theirs_kernel(hidden_far, after, out_far, parts, out, sems):
    half = 1 - lax.axis_index("xl")
    pack_hidden(half, start_hidden(hidden_far, parts, sems), parts, out, out_far, sems)


def values_kernel(
    momentum_far, gradient_far, indices_far, counts_far, table_far, hidden_far, sent, mine_far,
    momentum, gradient, indices, counts, table, parts, mine, sems, hidden_sems,
):
    copies = fetch(
        (indices_far, table_far.at[pl.ds(WIDE_T, 2)], momentum_far, gradient_far, counts_far), (indices, table, momentum, gradient, counts), sems
    )
    half = lax.axis_index("xl")
    hidden_copies = start_hidden(hidden_far, parts, hidden_sems)
    tiles = momentum.shape[1]
    copies[0].wait()
    copies[1].wait()
    line = index_line(indices)
    rows, columns = cosines(line, table)
    high, low = split(columns)
    lane = lax.broadcasted_iota(jnp.int32, (1, SIDE), 1)
    for copy in copies[2:]:
        copy.wait()
    out = []
    for t in range(tiles):
        e = slice(t * SIDE, t * SIDE + SIDE)
        moment = decay_rate * momentum[0, t] + gradient[0, t].astype(f32)
        mixed = dot3(split(moment), (high[:, e], low[:, e]))
        value = jnp.sum(mixed * rows[:, e], axis=0, keepdims=True)
        live = (lane & 31) < jnp.where(lane < 32, counts[2 * t], counts[2 * t + 1])
        out.append(jnp.concatenate([jnp.where(live, value, 0.0), line[:, e].astype(f32)], axis=1))
    out.append(jnp.zeros((sent.shape[1] - tiles, PAIR), f32))
    out = jnp.concatenate(out, axis=0)
    for r in range(sent.shape[0]):
        sent[r] = out
    pack_hidden(half, hidden_copies, parts, mine, mine_far, hidden_sems)


def momentum_kernel(momentum, gradient, indices, sent, table, out):
    tiles = momentum.shape[1]
    line = index_line(indices)
    rows, columns = cosines(line, table)
    high, low = split(columns)
    for t in range(tiles):
        e = slice(t * SIDE, t * SIDE + SIDE)
        moment = decay_rate * momentum[0, t] + gradient[0, t].astype(f32)
        weighted = rows[:, e] * sent[0, t : t + 1, :SIDE]
        out[0, t] = moment - dot3(split(weighted), (high[:, e], low[:, e]), ((1,), (1,)))


def shared_directions(got, tiles, first_row, rows, table):
    replicas, nt = got.shape[0], ((1,), (1,))
    wide_t = [table[i, pl.ds(first_row, rows), :SIDE] for i in (WIDE_T, WIDE_T + 1)]
    halves, sums = [], []
    for t in tiles:
        lines = [got[r, pl.ds(t, 1), :] for r in range(replicas)]
        values = jnp.concatenate([line[:, :SIDE] for line in lines], axis=1)
        indices = jnp.concatenate([line[:, SIDE:] for line in lines], axis=1).astype(jnp.int32)
        row_hot, column_hot = one_hots(indices)
        column_hot = jnp.where(column_hot, 1.0, 0.0).astype(bf16)
        weighted = split(jnp.where(row_hot, values, 0.0))
        shared = (dot(weighted[0], column_hot, nt) + dot(weighted[1], column_hot, nt)) / replicas
        sums.append(jnp.sum(shared * shared, axis=0, keepdims=True))
        halves.append(dot3(wide_t, split(shared)))
    raw = dot3(split(jnp.concatenate(halves, axis=0)), (table[WIDE], table[WIDE + 1]))
    high, low = split(jnp.concatenate(sums, axis=0))
    energy = dot(high, table[BLOCK_ONES]) + dot(low, table[BLOCK_ONES])
    scale = jnp.sqrt(energy / (SIDE * SIDE) + tiny_eps)
    return jnp.tanh(raw.reshape(len(tiles), rows, PAIR) / scale[:, None, :])


def new_weight_kernel(got, weight, table, pieces):
    count = pieces.shape[1]
    first_tile = lax.axis_index("xl") * count
    first_row = pl.multiple_of(lax.axis_index("y") * 16, 16)
    tiles = [first_tile + t for t in range(count)]
    moved = shared_directions(got, tiles, first_row, 16, table).astype(bf16).astype(f32)
    for t in range(count):
        old = weight[tiles[t], pl.ds(first_row, 16), :].astype(f32)
        new = (old - step_size * moved[t]).astype(bf16)
        for z in range(pieces.shape[0]):
            pieces[z, t] = new


def update_kernel(got, table, update):
    first_row = pl.multiple_of((lax.axis_index("xl") * 4 + lax.axis_index("y")) * 8, 8)
    rows = pl.multiple_of(first_row // 16 * 16, 16)
    tanhs = shared_directions(got, list(range(update.shape[0])), rows, 16, table)
    upper = first_row == rows
    update[...] = jnp.where(upper, tanhs[:, :8], tanhs[:, 8:]).astype(bf16)


def fill_kernel(source, matrix):
    xl = lax.axis_index("xl")
    for z in range(16):
        for t in range(5):
            start = z % 4 * 256 + t * 64 if t < 4 else 1024 + z % 4 * 64
            tile = t + xl if t < 4 else 4 - 4 * xl
            for y in range(4):
                row = start + y * 16
                matrix[row : row + 16, z // 4 * 128 : z // 4 * 128 + 128] = source[y, z, tile]


def fetch_rows(tokens, start, rows, sems):
    return fetch([t.at[:, pl.ds(start, HALF)] for t in tokens], [rows.at[s] for s in range(4)], sems)


def project_own_kernel(mine, xh_side, xl_side, across, matrix, total, later, rows, sems):
    tokens = mine, xh_side, xl_side, across
    copies = fetch_rows(tokens, 0, rows, sems)
    rest = fetch_rows(tokens, HALF, later, [sems.at[4 + s] for s in range(4)])
    for s in range(4):
        copies[s].wait()
        total[s] = jnp.dot(rows[s], matrix[...], preferred_element_type=f32)
    for copy in rest:
        copy.wait()


def project_rest_kernel(rows, matrix, total, out, block, out_sems):
    xl, xh = lax.axis_index("xl"), lax.axis_index("xh")
    slots = xl * 2 + xh, xl * 2 + 1 - xh, (1 - xl) * 2 + xh, (1 - xl) * 2 + 1 - xh
    leaving = []
    for s in range(4):
        whole = total[s] + jnp.dot(rows[s], matrix[...], preferred_element_type=f32)
        block[s] = whole.astype(bf16)
        leaving += fetch([block.at[s]], [out.at[slots[s]]], [out_sems.at[s]])
    for copy in leaving:
        copy.wait()


def combine_kernel(back, keys):
    for xh in range(2):
        whole = back[xh].astype(f32) + back[2 + xh].astype(f32)
        keys[:, xh * 512 : xh * 512 + 512] = whole.astype(bf16)


def call(kernel, out_shape, *args, scratch=(), flops=0, moved=0, limit=VMEM_LIMIT, **more):
    return pl.pallas_call(
        kernel,
        out_shape=out_shape,
        scratch_shapes=list(scratch),
        compiler_params=pltpu.CompilerParams(vmem_limit_bytes=limit),
        cost_estimate=pl.CostEstimate(flops=flops, bytes_accessed=moved, transcendentals=0),
        **more,
    )(*args)


def shards(hidden, weight, momentum, gradient, indices, counts):
    tiles = weight.shape[0]
    table = jnp.asarray(tables())
    vm, far = (pl.BlockSpec(memory_space=m) for m in (pltpu.VMEM, pltpu.HBM))
    shape = jax.ShapeDtypeStruct
    dmas = pltpu.SemaphoreType.DMA

    def room(*arrays):
        return [pltpu.VMEM(a.shape, a.dtype) for a in arrays]

    lines = indices.reshape(2 * tiles, 1, indices.shape[2])
    with jax.named_scope("own_values"):
        packing = room(hidden) + [pltpu.VMEM((256, 2 * HALF), bf16)]
        sent, mine = call(
            values_kernel,
            (shape((8, 16, PAIR), f32), shape((256, 2 * HALF), bf16)),
            momentum, gradient, lines, counts[0], table, hidden,
            scratch=room(momentum, gradient, lines) + [pltpu.SMEM((2 * tiles,), jnp.int32), pltpu.VMEM((2, PAIR, PAIR), bf16)] + packing + [dmas((5,)), dmas((8,))],
            moved=2**19,
            limit=MOST,
            in_specs=[far] * 6,
            out_specs=(vm, far),
        )

    with jax.named_scope("replica_exchange"):
        got = lax.all_to_all(sent, ("xl", "y"), 0, 0)

    with jax.named_scope("hidden_exchange"):
        swap, cross = [(0, 1), (1, 0)], [(0, 3), (1, 2), (2, 1), (3, 0)]
        xh_side = lax.ppermute(mine, "xh", swap)
        theirs = call(
            pack_theirs_kernel,
            shape((256, 2 * HALF), bf16),
            hidden, got,
            scratch=packing + [dmas((8,))],
            moved=2**22,
            limit=MOST,
            in_specs=[far, pl.BlockSpec(memory_space=pl.ANY)],
            out_specs=far,
        )
        xl_side = lax.ppermute(theirs, "xl", swap)
        across = lax.ppermute(theirs, ("xl", "xh"), cross)

    with jax.named_scope("new_weight"):
        pieces = call(
            new_weight_kernel,
            shape((16, tiles // 2, 16, PAIR), bf16),
            got, weight, table,
            flops=OWN_FLOPS,
            in_specs=[vm] * 3,
            out_specs=vm,
        )
        update = call(
            update_kernel,
            shape((tiles, 8, PAIR), bf16),
            got, table,
            moved=2**19,
            in_specs=[vm] * 2,
            out_specs=vm,
        )

    with jax.named_scope("weight_exchange"):
        along_z = lax.all_to_all(pieces, "z", 0, 0)
        along_z, xh_side = lax.optimization_barrier((along_z, xh_side))
        along_y = lax.all_to_all(jnp.broadcast_to(along_z, (4,) + along_z.shape), "y", 0, 0)
        matrix = shape((HALF, 512), bf16)
        own = call(fill_kernel, matrix, along_y, in_specs=[vm], out_specs=vm)
        other = lax.ppermute(own, "c", swap)

    with jax.named_scope("projection"):
        anywhere, half_rows = pl.BlockSpec(memory_space=pl.ANY), (4, 256, HALF)
        total, later = call(
            project_own_kernel,
            (shape((4, 256, 512), f32), shape(half_rows, bf16)),
            mine, xh_side, xl_side, across, own,
            scratch=[pltpu.VMEM(half_rows, bf16), dmas((8,))],
            flops=OWN_FLOPS,
            in_specs=[anywhere] * 4 + [vm],
            out_specs=(vm, vm),
        )
        partial = call(
            project_rest_kernel,
            shape((4, 256, 512), bf16),
            later, other, total,
            scratch=[pltpu.VMEM((4, 256, 512), bf16), dmas((4,))],
            in_specs=[vm] * 3,
            out_specs=far,
        )

    with jax.named_scope("output_exchange"):
        back = lax.all_to_all(partial, ("xl", "xh"), 0, 0)
        keys = call(combine_kernel, shape((256, 1024), bf16), back, in_specs=[vm], out_specs=vm)

    with jax.named_scope("momentum"):
        new_momentum = call(
            momentum_kernel,
            shape(momentum.shape, f32),
            momentum, gradient, lines, sent, table,
            moved=2**20,
            in_specs=[vm] * 5,
            out_specs=vm,
        )
    return (keys, update, new_momentum)


def solution(mesh):
    fine = Mesh(mesh.devices.reshape(2, 4, 2, 16, 2), axes)
    rep, group = ("xl", "y"), ("xh", "z", "c")
    in_specs = (
        P(axes, None),
        P(group, None, None),
        P(rep, group, None, None),
        P(rep, group, None, None),
        P(rep, group, None),
        P(rep, group),
    )
    out_specs = (P(axes, None), P(group, rep, None), P(rep, group, None, None))
    return jax.shard_map(shards, mesh=fine, in_specs=in_specs, out_specs=out_specs, check_vma=False)
```
